256 devices in a mesh: dom: 64 (over z, y, core), space: 4 (over x).
Axes of the slice: x: 4, y: 4, z: 8, core: 2. Of those that a mesh axis runs over, the one named last changes fastest.
Arguments:
- ensemble: float32 [64, 2, 32, 4096], P('dom', None, 'space'), may hold values from -6 to 6
- offspring: int32 [64], replicated, may hold values from 0 to 16, as said below
- new_owner: int32 [64], replicated, may hold values from 0 to 63, as said below
- perturb: bfloat16 [64, 2, 2, 32, 4096], P('dom', None, None, 'space'), may hold values from -6 to 6
- observed: float32 [32, 4096], P('space'), may hold values from -6 to 6
- nudge_rate: float32 [32], P('space'), may hold values from 1 to 10
Outputs:
- analysis: float32 [64, 2, 32, 4096], P('dom', None, 'space')
The draws below stay inside these ranges and needn't reach their ends.
Inputs may be any that keep to these rules, and one draw needn't show every extreme that they name: The counts sum to 64; at most 4 particles have more than one offspring. A permutation. Copies are listed parent by parent in increasing order of the parent; copy j becomes member new_owner[j], and the first copy of every particle with offspring becomes that particle's own member.
All inputs are finite; a program needn't handle non-finite values.
Results may differ from the reference program's by a relative error of at most 0.0003.
Values sent between devices are 32-bit elements; how exact they have to be, the bound alone decides.
A program may use at most 64 MiB of HBM per device.

```python
import math
import jax
import jax.numpy as jnp
from jax import lax

COLS = 4096
STEPS = 2
SWEEPS = 2
HEAVY = 4
PARTICLES = 64
MOST = 16
NY = 32


def shared_plan(key):
    order_key = jax.random.fold_in(key, 11)
    count_key = jax.random.fold_in(key, 12)
    empty_key = jax.random.fold_in(key, 13)
    shuffled = jax.random.permutation(order_key, PARTICLES).astype(jnp.int32)
    heavy_counts = jax.random.randint(count_key, (HEAVY,), 2, MOST + 1).astype(jnp.int32)
    heavy_counts = heavy_counts.at[0].set(MOST)
    singles = PARTICLES - jnp.sum(heavy_counts)
    ranking = jnp.arange(PARTICLES, dtype=jnp.int32)
    sorted_counts = jnp.where(ranking < HEAVY, heavy_counts[jnp.minimum(ranking, HEAVY - 1)], jnp.where(ranking < HEAVY + singles, 1, 0)).astype(jnp.int32)
    offspring = jnp.zeros((PARTICLES,), jnp.int32).at[shuffled].set(sorted_counts)
    cumulative = jnp.cumsum(offspring).astype(jnp.int32)
    earlier = cumulative - offspring
    parent_copy = jnp.searchsorted(cumulative, ranking, side='right').astype(jnp.int32)
    first_copy = ranking == earlier[parent_copy]
    extra_rank = jnp.cumsum((~first_copy).astype(jnp.int32)) - 1
    scores = jnp.where(offspring == 0, jax.random.permutation(empty_key, PARTICLES).astype(jnp.int32), PARTICLES + ranking)
    empty_order = jnp.argsort(scores, stable=True).astype(jnp.int32)
    owners = jnp.where(first_copy, parent_copy, empty_order[jnp.clip(extra_rank, 0, PARTICLES - 1)])
    return (offspring, owners.astype(jnp.int32))


def draw_offspring(key, part):
    counts, owners = shared_plan(key)
    return counts


def draw_new_owner(key, part):
    counts, owners = shared_plan(key)
    return owners


def level_of(rng, dims, shards, smallest, top_value):
    def one(axis_at, shards_of):
        steps = jax.random.uniform(jax.random.fold_in(jax.random.fold_in(rng, 6), axis_at), (shards_of,), jnp.float32, smallest / len(shards), top_value / len(shards))
        return jnp.repeat(jnp.exp(steps), dims[axis_at] // shards_of).reshape((-1,) + (1,) * (len(dims) - axis_at - 1))

    level = one(*shards[0])
    for cut in shards[1:]:
        level = level * one(*cut)
    return level


def noise(rng, shape, scale, reach, pieces=(), kind=jnp.bfloat16):
    drawn = scale * jax.random.normal(rng, shape, jnp.float32)
    if pieces:
        drawn = drawn * level_of(rng, shape, pieces, -0.22, 0.18)
    return jnp.clip(drawn, -reach, reach).astype(kind)


def setup_inputs(seed: int = 0) -> dict:
    seeds = jax.random.split(jax.random.key(seed), 7)
    ensemble = noise(seeds[0], (PARTICLES, 2, NY, COLS), 1.0, 6.0, ((0, 64), (2, 4)), jnp.float32)
    offspring = draw_offspring(jax.random.fold_in(seeds[6], 71), 0)
    new_owner = draw_new_owner(jax.random.fold_in(seeds[6], 71), 0)
    perturb = noise(seeds[3], (PARTICLES, STEPS, 2, NY, COLS), 1.0, 6.0, ((0, 64), (3, 4)))
    observed = noise(seeds[4], (NY, COLS), 1.0, 6.0, ((0, 4),), jnp.float32)
    nudge_rate = jnp.clip(jnp.exp(math.log(10.0) - 2.3025851 * jax.random.uniform(seeds[5], (NY,), jnp.float32) ** level_of(seeds[5], (NY,), ((0, 4),), -0.2, 0.2)), 1.0, 10.0)
    return dict(ensemble=ensemble, offspring=offspring, new_owner=new_owner, perturb=perturb, observed=observed, nudge_rate=nudge_rate)


time_step = 0.05
beta_plane = 1.0
noise_scale = 0.5


def layer_coupling():
    return jnp.array([0.4, 0.6], dtype=jnp.float32)[:, None, None]


def bottom_drag():
    return jnp.array([0.0, 0.2], dtype=jnp.float32)[:, None, None]


def laplace(values):
    padded = jnp.pad(values, ((0, 0), (1, 1), (0, 0)))
    return padded[:, 2:] + padded[:, :-2] + jnp.roll(values, 1, 2) + jnp.roll(values, -1, 2) - 4.0 * values


def coupling(values):
    return layer_coupling() * (values[::-1] - values)


def model_step(stream, perturb_now, observed, nudge_rate):
    potential = laplace(stream) + coupling(stream)
    stream_pad = jnp.pad(stream, ((0, 0), (1, 1), (0, 0)))
    potential_pad = jnp.pad(potential, ((0, 0), (1, 1), (0, 0)))
    east_stream = jnp.roll(stream, -1, 2) - jnp.roll(stream, 1, 2)
    north_stream = stream_pad[:, 2:] - stream_pad[:, :-2]
    east_pot = jnp.roll(potential, -1, 2) - jnp.roll(potential, 1, 2)
    north_pot = potential_pad[:, 2:] - potential_pad[:, :-2]
    advection = (east_stream * north_pot - north_stream * east_pot) / 4.0
    tendency = -advection - beta_plane * 0.5 * east_stream - bottom_drag() * potential
    upper = time_step * nudge_rate[:, None] * (observed - stream[0])
    nudging = jnp.stack([upper, jnp.zeros_like(upper)])
    target = potential + time_step * tendency + nudging + noise_scale * perturb_now.astype(jnp.float32)
    diagonal = 4.0 + layer_coupling()
    for sweep_no in range(SWEEPS):
        stream = stream + (laplace(stream) + coupling(stream) - target) / diagonal
    return stream


def reference(ensemble, offspring, new_owner, perturb, observed, nudge_rate):
    cumulative = jnp.cumsum(offspring).astype(jnp.int32)
    copy_index = jnp.arange(PARTICLES, dtype=jnp.int32)
    parent_copy = jnp.searchsorted(cumulative, copy_index, side="right").astype(jnp.int32)
    parent_slot = jnp.zeros((PARTICLES,), jnp.int32).at[new_owner].set(parent_copy)
    chosen = ensemble[parent_slot]

    def advance(paired):
        stream, member_noise = paired
        for step_no in range(STEPS):
            stream = model_step(stream, member_noise[step_no], observed, nudge_rate)
        return stream

    return lax.map(advance, (chosen, perturb))
```

```python
import functools

import jax
import jax.numpy as jnp
from jax import lax
from jax.experimental import pallas as pl
from jax.experimental.pallas import tpu as pltpu
from jax.sharding import PartitionSpec as P

STEPS = 2
COLS = 4096
ROWS = 8
MEMBERS = 64
LANES = 128
CHUNK = 512
COUPLE = (0.4, 0.6)
DRAG = (0.0, 0.2)
DT = 0.05
BETA = 1.0
NOISE = 0.5
F32 = jnp.float32


def sublane(shape):
    return lax.broadcasted_iota(jnp.int32, shape, len(shape) - 2)


def tile_of(device):
    return lax.rem(device, 2), pl.multiple_of(lax.div(device, 2) * LANES, LANES)


def partner(step, me):
    group, within = lax.div(step, 8), lax.rem(lax.rem(step, 8) + 1, 8)
    spread = lax.div(group + 1, 2)
    dz = jnp.where(lax.rem(group, 2) == 1, 4 - spread, 4 + spread)
    z, y, core = lax.div(me, 8), lax.rem(lax.div(me, 2), 4), lax.rem(me, 2)
    z = lax.rem(z + dz, 8)
    y = lax.rem(y + lax.div(within, 2), 4)
    core = lax.rem(core + lax.rem(within, 2), 2)
    return (z * 4 + y) * 2 + core


def window(ref, layer, start):
    left = pl.multiple_of(lax.rem(start + COLS - LANES, COLS), LANES)
    right = pl.multiple_of(lax.rem(start + CHUNK, COLS), LANES)
    return (
        ref[layer, :, pl.ds(left, LANES)],
        ref[layer, :, pl.ds(start, CHUNK)],
        ref[layer, :, pl.ds(right, LANES)],
    )


def west(parts):
    both = jnp.concatenate([parts[0], parts[1]], axis=1)
    return pltpu.roll(both, 1, 1)[:, LANES:]


def east(parts):
    both = jnp.concatenate([parts[1], parts[2]], axis=1)
    return pltpu.roll(both, CHUNK + LANES - 1, 1)[:, :CHUNK]


def up_of(value):
    return pltpu.roll(value, 1, 0)


def down_of(value):
    return pltpu.roll(value, ROWS - 1, 0)


def rows_beside(own, halo, outer):
    at = sublane(own.shape)
    up_o, up_h, down_o, down_h = up_of(own), up_of(halo), down_of(own), down_of(halo)
    above_o = jnp.where(at == 0, up_h, up_o)
    below_o = jnp.where(at == 7, down_h, down_o)
    above_h = jnp.where(at == 0, up_o, up_h)
    below_h = jnp.where(at == 7, down_o, down_h)
    if outer is None:
        return (above_o, above_h), (below_o, below_h)
    up_t, down_t = up_of(outer), down_of(outer)
    above_h = jnp.where(at == 4, up_t, above_h)
    below_h = jnp.where(at == 3, down_t, below_h)
    above_t = jnp.where(at == 4, up_h, up_t)
    below_t = jnp.where(at == 3, down_h, down_t)
    return (above_o, above_h, above_t), (below_o, below_h, below_t)


def laplace(parts, above, below):
    return above + below + west(parts) + east(parts) - 4.0 * parts[1]


def model_step(s, q, target, s1, force, pull, inside, step_no, last):
    n_q = 2 if last else 3
    chunks = COLS // CHUNK

    def vorticity(k, carry):
        start = pl.multiple_of(k * CHUNK, CHUNK)
        parts = [[window(s[i], layer, start) for i in range(n_q)] for layer in range(2)]
        for layer in range(2):
            mine = parts[layer]
            centre = [p[1] for p in mine] + [None] * (3 - n_q)
            above, below = rows_beside(*centre)
            for i in range(n_q):
                value = laplace(mine[i], above[i], below[i]) + COUPLE[layer] * (
                    parts[1 - layer][i][1] - mine[i][1]
                )
                if i:
                    value = jnp.where(inside, value, 0.0)
                q[i][layer, :, pl.ds(start, CHUNK)] = value
        return carry

    def first_sweep(k, carry):
        start = pl.multiple_of(k * CHUNK, CHUNK)
        here = pl.ds(start, CHUNK)
        for layer in range(2):
            s_parts = [window(s[i], layer, start) for i in range(2)]
            q_parts = [window(q[i], layer, start) for i in range(2)]
            s_outer = None if last else s[2][layer, :, here]
            q_outer = None if last else q[2][layer, :, here]
            s_above, s_below = rows_beside(s_parts[0][1], s_parts[1][1], s_outer)
            q_above, q_below = rows_beside(q_parts[0][1], q_parts[1][1], q_outer)
            for i in range(2):
                state, vort = s_parts[i][1], q_parts[i][1]
                ex_s = east(s_parts[i]) - west(s_parts[i])
                ex_q = east(q_parts[i]) - west(q_parts[i])
                ny_s = s_below[i] - s_above[i]
                ny_q = q_below[i] - q_above[i]
                tendency = (ny_s * ex_q - ex_s * ny_q) * 0.25 - (BETA * 0.5) * ex_s
                if DRAG[layer]:
                    tendency = tendency - DRAG[layer] * vort
                change = DT * tendency + force[i][step_no, layer, :, here]
                if layer == 0:
                    change = change - pull[i][:, 0:1] * state
                target[i][layer, :, here] = vort + change
                value = state - change * (1.0 / (4.0 + COUPLE[layer]))
                if i:
                    value = jnp.where(inside, value, 0.0)
                s1[i][layer, :, here] = value
        return carry

    def second_sweep(k, carry):
        start = pl.multiple_of(k * CHUNK, CHUNK)
        here = pl.ds(start, CHUNK)
        parts = [[window(s1[i], layer, start) for i in range(2)] for layer in range(2)]
        for layer in range(2):
            mine = parts[layer]
            above, below = rows_beside(mine[0][1], mine[1][1], None)
            for i in range(1 if last else 2):
                centre = mine[i][1]
                rest = (
                    laplace(mine[i], above[i], below[i])
                    + COUPLE[layer] * (parts[1 - layer][i][1] - centre)
                    - target[i][layer, :, here]
                )
                value = centre + rest * (1.0 / (4.0 + COUPLE[layer]))
                if i:
                    value = jnp.where(inside, value, 0.0)
                s[i][layer, :, here] = value
        return carry

    lax.fori_loop(0, chunks, vorticity, 0)
    lax.fori_loop(0, chunks, first_sweep, 0)
    lax.fori_loop(0, chunks, second_sweep, 0)


def kernel(
    offspring, new_owner, nudge, ensemble, perturb, observed, out,
    own_state, noise, obs, tiles, picked, parent_row, parent_at,
    s_own, s_halo, s_outer, q_own, q_halo, q_outer, s1_own, s1_halo,
    target_own, target_halo, force_own, force_halo, pull_own, pull_halo,
    local_sem, send_sem, recv_sem, row_send, row_recv,
):
    me, x = lax.axis_index("dom"), lax.axis_index("space")
    next_x, prev_x = lax.rem(x + 1, 4), lax.rem(x + 3, 4)

    loads = [
        pltpu.make_async_copy(ensemble.at[0], own_state, local_sem.at[0]),
        pltpu.make_async_copy(perturb.at[0], noise, local_sem.at[1]),
        pltpu.make_async_copy(observed, obs, local_sem.at[2]),
    ]
    for load in loads:
        load.start()

    barrier = pltpu.get_barrier_semaphore()

    def greet(step, carry):
        pl.semaphore_signal(barrier, inc=1, device_id=(partner(step, me), x))
        return carry

    lax.fori_loop(0, MEMBERS - 1, greet, 0)
    pl.semaphore_signal(barrier, inc=1, device_id=(me, next_x))
    pl.semaphore_signal(barrier, inc=1, device_id=(me, prev_x))

    lane = lax.broadcasted_iota(jnp.int32, (8, LANES), 1)

    def find_copy(j, copy):
        return jnp.where(lane == new_owner[j], j, copy)

    copy = lax.fori_loop(0, MEMBERS, find_copy, jnp.zeros((8, LANES), jnp.int32))

    def find_parent(i, carry):
        total, parent = carry
        total = total + offspring[i]
        return total, parent + (total <= copy).astype(jnp.int32)

    _, parent = lax.fori_loop(
        0, MEMBERS, find_parent, (jnp.int32(0), jnp.zeros((8, LANES), jnp.int32))
    )
    parent_row[...] = jnp.minimum(parent, MEMBERS - 1)
    to_scalars = pltpu.make_async_copy(parent_row, parent_at, local_sem.at[3])
    to_scalars.start()

    at = sublane((ROWS, LANES))
    rate = jnp.zeros((ROWS, LANES), F32)
    for r in range(ROWS):
        rate = jnp.where(at == r, DT * nudge[r], rate)
    pull_own[...] = rate
    loads[1].wait()
    loads[2].wait()

    def forcing(k, carry):
        here = pl.ds(pl.multiple_of(k * CHUNK, CHUNK), CHUNK)
        drawn = rate[:, 0:1] * obs[:, here]
        for t in range(STEPS):
            for layer in range(2):
                value = NOISE * noise[t, layer, :, here].astype(F32)
                force_own[t, layer, :, here] = value + drawn if layer == 0 else value
        return carry

    lax.fori_loop(0, COLS // CHUNK, forcing, 0)
    loads[0].wait()
    pl.semaphore_wait(barrier, MEMBERS + 1)

    def spread(step, carry):
        to = partner(step, me)
        layer, start = tile_of(to)
        pltpu.make_async_remote_copy(
            src_ref=own_state.at[layer, :, pl.ds(start, LANES)],
            dst_ref=tiles.at[me],
            send_sem=send_sem.at[0],
            recv_sem=recv_sem.at[0],
            device_id=(to, x),
        ).start()
        return carry

    lax.fori_loop(0, MEMBERS - 1, spread, 0)

    def row_copy(src, dst, number, to_x):
        return pltpu.make_async_remote_copy(
            src_ref=src,
            dst_ref=dst,
            send_sem=row_send.at[number],
            recv_sem=row_recv.at[number],
            device_id=(me, to_x),
        )

    low, high = pl.ds(0, 4), pl.ds(4, 4)
    early = [
        row_copy(force_own.at[0, :, low], force_halo.at[0, :, low], 0, prev_x),
        row_copy(force_own.at[0, :, high], force_halo.at[0, :, high], 1, next_x),
        row_copy(force_own.at[1, :, pl.ds(0, 1)], force_halo.at[1, :, pl.ds(0, 1)], 2, prev_x),
        row_copy(force_own.at[1, :, pl.ds(7, 1)], force_halo.at[1, :, pl.ds(7, 1)], 3, next_x),
        row_copy(pull_own.at[low], pull_halo.at[low], 4, prev_x),
        row_copy(pull_own.at[high], pull_halo.at[high], 5, next_x),
    ]
    for one in early:
        one.start()

    my_layer, my_start = tile_of(me)
    tiles[me] = own_state[my_layer, :, pl.ds(my_start, LANES)]
    to_scalars.wait()

    def all_tiles(sem):
        return pltpu.make_async_copy(
            tiles.at[pl.ds(0, MEMBERS - 1)], tiles.at[pl.ds(0, MEMBERS - 1)], sem
        )

    all_tiles(recv_sem.at[0]).wait()

    def choose(m, carry):
        picked[m] = tiles[parent_at[0, m]]
        return carry

    lax.fori_loop(0, MEMBERS, choose, 0)

    def deliver(step, carry):
        to = partner(step, me)
        pltpu.make_async_remote_copy(
            src_ref=picked.at[to],
            dst_ref=s_own.at[my_layer, :, pl.ds(my_start, LANES)],
            send_sem=send_sem.at[1],
            recv_sem=recv_sem.at[1],
            device_id=(to, x),
        ).start()
        return carry

    lax.fori_loop(0, MEMBERS - 1, deliver, 0)
    s_own[my_layer, :, pl.ds(my_start, LANES)] = picked[me]
    all_tiles(recv_sem.at[1]).wait()

    states = [
        row_copy(s_own.at[:, low], s_halo.at[:, low], 6, prev_x),
        row_copy(s_own.at[:, high], s_halo.at[:, high], 7, next_x),
        row_copy(s_own.at[:, pl.ds(4, 2)], s_outer.at[:, pl.ds(4, 2)], 8, prev_x),
        row_copy(s_own.at[:, pl.ds(2, 2)], s_outer.at[:, pl.ds(2, 2)], 9, next_x),
    ]
    for one in states:
        one.start()
    all_tiles(send_sem.at[0]).wait()
    all_tiles(send_sem.at[1]).wait()
    for one in early + states:
        one.wait()

    wide = sublane((ROWS, CHUNK))
    inside = jnp.where(wide < 4, jnp.where(x < 3, 1, 0), jnp.where(x > 0, 1, 0)) == 1

    def clear(k, carry):
        here = pl.ds(pl.multiple_of(k * CHUNK, CHUNK), CHUNK)
        for layer in range(2):
            for ref in (s_halo, s_outer):
                ref[layer, :, here] = jnp.where(inside, ref[layer, :, here], 0.0)
        return carry

    lax.fori_loop(0, COLS // CHUNK, clear, 0)

    s, q = (s_own, s_halo, s_outer), (q_own, q_halo, q_outer)
    target, s1 = (target_own, target_halo), (s1_own, s1_halo)
    force, pull = (force_own, force_halo), (pull_own, pull_halo)
    for t in range(STEPS):
        model_step(s, q, target, s1, force, pull, inside, t, t == STEPS - 1)

    result = pltpu.make_async_copy(s_own, out.at[0], local_sem.at[0])
    result.start()
    result.wait()


def per_device(ensemble, offspring, new_owner, perturb, observed, nudge_rate):
    layers = pltpu.VMEM((2, ROWS, COLS), F32)
    forces = pltpu.VMEM((STEPS, 2, ROWS, COLS), F32)
    small = pltpu.VMEM((ROWS, LANES), F32)
    tiles = pltpu.VMEM((MEMBERS, 8, LANES), F32)
    return pl.pallas_call(
        kernel,
        out_shape=jax.ShapeDtypeStruct(ensemble.shape, F32),
        in_specs=[pl.BlockSpec(memory_space=pltpu.SMEM)] * 3
        + [pl.BlockSpec(memory_space=pl.ANY)] * 3,
        out_specs=pl.BlockSpec(memory_space=pl.ANY),
        scratch_shapes=[
            layers,
            pltpu.VMEM((STEPS, 2, ROWS, COLS), jnp.bfloat16),
            pltpu.VMEM((ROWS, COLS), F32),
            tiles,
            tiles,
            pltpu.VMEM((8, LANES), jnp.int32),
            pltpu.SMEM((8, LANES), jnp.int32),
            *[layers] * 10,
            forces,
            forces,
            small,
            small,
            pltpu.SemaphoreType.DMA((4,)),
            pltpu.SemaphoreType.DMA((2,)),
            pltpu.SemaphoreType.DMA((2,)),
            pltpu.SemaphoreType.DMA((10,)),
            pltpu.SemaphoreType.DMA((10,)),
        ],
        compiler_params=pltpu.CompilerParams(
            collective_id=0, has_side_effects=True, vmem_limit_bytes=32 * 1024 * 1024
        ),
        name="filter_step",
    )(offspring, new_owner, nudge_rate, ensemble, perturb, observed)


def solution(mesh):
    in_specs = (
        P("dom", None, "space", None),
        P(),
        P(),
        P("dom", None, None, "space", None),
        P("space", None),
        P("space"),
    )
    out_specs = P("dom", None, "space", None)
    return jax.shard_map(
        per_device, mesh=mesh, in_specs=in_specs, out_specs=out_specs, check_vma=False
    )
```

```python
import functools

import jax
import jax.numpy as jnp
from jax import lax
from jax.experimental import pallas as pl
from jax.experimental.pallas import tpu as pltpu
from jax.sharding import PartitionSpec as P

STEPS = 2
COLS = 4096
ROWS = 8
MEMBERS = 64
LANES = 128
PLANES = 8
PER_PLANE = 8
BAND = COLS // PLANES
PARTS = ((0, 4), (4, 4))
COUPLE = (0.4, 0.6)
DRAG = (0.0, 0.2)
DT = 0.05
BETA = 1.0
NOISE = 0.5
F32 = jnp.float32


def sublane(shape):
    return lax.broadcasted_iota(jnp.int32, shape, len(shape) - 2)


def west(value):
    return pltpu.roll(value, 1, 1)


def east(value):
    return pltpu.roll(value, COLS - 1, 1)


def up_of(value):
    return pltpu.roll(value, 1, 0)


def down_of(value):
    return pltpu.roll(value, ROWS - 1, 0)


def rows_beside(own, halo, outer):
    at = sublane(own.shape)
    up_o, up_h, down_o, down_h = up_of(own), up_of(halo), down_of(own), down_of(halo)
    above_o = jnp.where(at == 0, up_h, up_o)
    below_o = jnp.where(at == 7, down_h, down_o)
    above_h = jnp.where(at == 0, up_o, up_h)
    below_h = jnp.where(at == 7, down_o, down_h)
    if outer is None:
        return (above_o, above_h), (below_o, below_h)
    up_t, down_t = up_of(outer), down_of(outer)
    above_h = jnp.where(at == 4, up_t, above_h)
    below_h = jnp.where(at == 3, down_t, below_h)
    above_t = jnp.where(at == 4, up_h, up_t)
    below_t = jnp.where(at == 3, down_h, down_t)
    return (above_o, above_h, above_t), (below_o, below_h, below_t)


def laplace(value, above, below):
    return above + below + west(value) + east(value) - 4.0 * value


def model_step(s, q, target, s1, force, pull, inside, step_no, last):
    n_q = 2 if last else 3

    mine = [[s[i][layer] for i in range(n_q)] for layer in range(2)]
    for layer in range(2):
        above, below = rows_beside(*mine[layer], *[None] * (3 - n_q))
        for i in range(n_q):
            here, other = mine[layer][i], mine[1 - layer][i]
            value = laplace(here, above[i], below[i]) + COUPLE[layer] * (other - here)
            q[i][layer] = jnp.where(inside, value, 0.0) if i else value

    for layer in range(2):
        state, vort = [s[i][layer] for i in range(2)], [q[i][layer] for i in range(2)]
        s_above, s_below = rows_beside(*state, None if last else s[2][layer])
        q_above, q_below = rows_beside(*vort, None if last else q[2][layer])
        for i in range(2):
            ex_s = east(state[i]) - west(state[i])
            ex_q = east(vort[i]) - west(vort[i])
            ny_s = s_below[i] - s_above[i]
            ny_q = q_below[i] - q_above[i]
            tendency = (ny_s * ex_q - ex_s * ny_q) * 0.25 - (BETA * 0.5) * ex_s
            if DRAG[layer]:
                tendency = tendency - DRAG[layer] * vort[i]
            change = DT * tendency + force[i][step_no, layer]
            if layer == 0:
                change = change - pull[i][:, 0:1] * state[i]
            target[i][layer] = vort[i] + change
            value = state[i] - change * (1.0 / (4.0 + COUPLE[layer]))
            s1[i][layer] = jnp.where(inside, value, 0.0) if i else value

    mine = [[s1[i][layer] for i in range(2)] for layer in range(2)]
    for layer in range(2):
        above, below = rows_beside(*mine[layer], None)
        for i in range(1 if last else 2):
            here, other = mine[layer][i], mine[1 - layer][i]
            rest = (
                laplace(here, above[i], below[i])
                + COUPLE[layer] * (other - here)
                - target[i][layer]
            )
            value = here + rest * (1.0 / (4.0 + COUPLE[layer]))
            s[i][layer] = jnp.where(inside, value, 0.0) if i else value


def kernel(
    offspring_in, new_owner_in, nudge_in, ensemble, perturb, observed, out,
    offspring, new_owner, nudge, noise, obs, tiles_a, tiles_b, picked_a, picked_b,
    parent_row, parent_at,
    s_own, s_halo, s_outer, q_own, q_halo, q_outer, s1_own, s1_halo,
    target_own, target_halo, force_own, force_halo, pull_own, pull_halo,
    local_sem, spread_send, spread_recv, deliver_send, deliver_recv,
    early_send, early_recv, row_send, row_recv,
):
    me, x = lax.axis_index("dom"), lax.axis_index("space")
    next_x, prev_x = lax.rem(x + 1, 4), lax.rem(x + 3, 4)
    plane, y, core = lax.div(me, 8), lax.rem(lax.div(me, 2), 4), lax.rem(me, 2)
    tiles, picked = (tiles_a, tiles_b), (picked_a, picked_b)
    places = [
        (lax.rem(y + dy, 4) * 2 + lax.rem(core + dc, 2), lax.rem(y + dy, 4), lax.rem(core + dc, 2))
        for dy, dc in ((2, 1), (2, 0), (1, 1), (1, 0), (3, 1), (3, 0), (0, 1), (0, 0))
    ]

    def nth_plane(n):
        half = lax.div(n + 1, 2)
        return lax.rem(plane + jnp.where(lax.rem(n, 2) == 1, 4 - half, 4 + half), PLANES)

    def for_partners(act):
        def one_plane(n, carry, count=PER_PLANE):
            z = nth_plane(n)
            for place, at_y, at_core in places[:count]:
                act(z * PER_PLANE + place, at_core, pl.multiple_of((z * 4 + at_y) * LANES, LANES))
            return carry

        lax.fori_loop(0, PLANES - 1, one_plane, 0)
        one_plane(PLANES - 1, 0, PER_PLANE - 1)

    loads = [
        pltpu.make_async_copy(new_owner_in, new_owner, local_sem.at[0]),
        pltpu.make_async_copy(offspring_in, offspring, local_sem.at[1]),
        pltpu.make_async_copy(nudge_in, nudge, local_sem.at[2]),
        pltpu.make_async_copy(perturb.at[0], noise, local_sem.at[3]),
        pltpu.make_async_copy(observed, obs, local_sem.at[4]),
    ]
    for load in loads:
        load.start()

    barrier = pltpu.get_barrier_semaphore()
    for_partners(
        lambda to, layer, start: pl.semaphore_signal(barrier, inc=1, device_id=(to, x))
    )
    pl.semaphore_signal(barrier, inc=1, device_id=(me, next_x))
    pl.semaphore_signal(barrier, inc=1, device_id=(me, prev_x))
    pl.semaphore_wait(barrier, MEMBERS + 1)

    my_start = pl.multiple_of(lax.div(me, 2) * LANES, LANES)
    own_tiles = []
    for part, (row, count) in enumerate(PARTS):
        rows = pl.ds(row, count)

        def spread(to, layer, start, part=part, rows=rows):
            pltpu.make_async_remote_copy(
                src_ref=ensemble.at[0, layer, rows, pl.ds(start, LANES)],
                dst_ref=tiles[part].at[me, rows],
                send_sem=spread_send.at[part],
                recv_sem=spread_recv.at[part],
                device_id=(to, x),
            ).start()

        for_partners(spread)
        own = pltpu.make_async_copy(
            ensemble.at[0, core, rows, pl.ds(my_start, LANES)],
            tiles[part].at[me, rows],
            local_sem.at[5 + part],
        )
        own.start()
        own_tiles.append(own)

    for load in loads:
        load.wait()
    lane = lax.broadcasted_iota(jnp.int32, (8, LANES), 1)
    copy = jnp.zeros((8, LANES), jnp.int32)
    for j in range(MEMBERS):
        copy = jnp.where(lane == new_owner[j], j, copy)
    parent, total = jnp.zeros((8, LANES), jnp.int32), jnp.int32(0)
    for i in range(MEMBERS):
        total = total + offspring[i]
        parent = parent + (total <= copy).astype(jnp.int32)
    parent_row[...] = jnp.minimum(parent, MEMBERS - 1)
    to_scalars = pltpu.make_async_copy(parent_row, parent_at, local_sem.at[0])
    to_scalars.start()

    at = sublane((ROWS, LANES))
    rate = jnp.zeros((ROWS, LANES), F32)
    for r in range(ROWS):
        rate = jnp.where(at == r, DT * nudge[r], rate)
    pull_own[...] = rate
    drawn = rate[:, 0:1] * obs[...]
    for t in range(STEPS):
        for layer in range(2):
            value = NOISE * noise[t, layer].astype(F32)
            force_own[t, layer] = value + drawn if layer == 0 else value

    def early_copy(src, dst, number, to_x):
        return pltpu.make_async_remote_copy(
            src_ref=src,
            dst_ref=dst,
            send_sem=early_send.at[number],
            recv_sem=early_recv.at[number],
            device_id=(me, to_x),
        )

    low, high = pl.ds(0, 4), pl.ds(4, 4)
    early = [
        early_copy(force_own.at[0, :, low], force_halo.at[0, :, low], 0, prev_x),
        early_copy(force_own.at[0, :, high], force_halo.at[0, :, high], 1, next_x),
        early_copy(force_own.at[1, :, pl.ds(0, 1)], force_halo.at[1, :, pl.ds(0, 1)], 2, prev_x),
        early_copy(force_own.at[1, :, pl.ds(7, 1)], force_halo.at[1, :, pl.ds(7, 1)], 3, next_x),
        early_copy(pull_own.at[low], pull_halo.at[low], 4, prev_x),
        early_copy(pull_own.at[high], pull_halo.at[high], 5, next_x),
    ]
    for one in early:
        one.start()
    to_scalars.wait()

    def tiles_of(part, count):
        some = tiles[part].at[pl.ds(0, count), pl.ds(*PARTS[part])]
        return lambda sem: pltpu.make_async_copy(some, some, sem).wait()

    for part, (row, count) in enumerate(PARTS):
        rows = pl.ds(row, count)
        own_tiles[part].wait()
        tiles_of(part, MEMBERS - 1)(spread_recv.at[part])
        for m in range(MEMBERS):
            picked[part][m, rows] = tiles[part][parent_at[0, m], rows]

        def deliver(to, layer, start, part=part, rows=rows):
            pltpu.make_async_remote_copy(
                src_ref=picked[part].at[to, rows],
                dst_ref=s_own.at[core, rows, pl.ds(my_start, LANES)],
                send_sem=deliver_send.at[part],
                recv_sem=deliver_recv.at[part, plane],
                device_id=(to, x),
            ).start()

        for_partners(deliver)
        s_own[core, rows, pl.ds(my_start, LANES)] = picked[part][me, rows]

    def forward(part, z):
        band = pl.ds(pl.multiple_of(z * BAND, BAND), BAND)
        sides = (
            ((low, s_halo, prev_x, 0), (pl.ds(2, 2), s_outer, next_x, 1)),
            ((high, s_halo, next_x, 2), (pl.ds(4, 2), s_outer, prev_x, 3)),
        )[part]
        for rows, halo, to_x, number in sides:
            pltpu.make_async_remote_copy(
                src_ref=s_own.at[:, rows, band],
                dst_ref=halo.at[:, rows, band],
                send_sem=row_send.at[number],
                recv_sem=row_recv.at[number],
                device_id=(me, to_x),
            ).start()

    for part in range(len(PARTS)):

        def pass_on(n, carry, part=part, count=PER_PLANE):
            z = nth_plane(n)
            tiles_of(part, count)(deliver_recv.at[part, z])
            forward(part, z)
            return carry

        lax.fori_loop(0, PLANES - 1, pass_on, 0)
        pass_on(PLANES - 1, 0, count=PER_PLANE - 1)

    for part in range(len(PARTS)):
        tiles_of(part, MEMBERS - 1)(spread_send.at[part])
        tiles_of(part, MEMBERS - 1)(deliver_send.at[part])
    for one in early:
        one.wait()
    for number, count in enumerate((4, 2, 4, 2)):
        some = s_own.at[:, pl.ds(0, count)]
        for sem in (row_recv, row_send):
            pltpu.make_async_copy(some, some, sem.at[number]).wait()

    wide = sublane((ROWS, COLS))
    inside = jnp.where(wide < 4, jnp.where(x < 3, 1, 0), jnp.where(x > 0, 1, 0)) == 1
    for ref in (s_halo, s_outer):
        for layer in range(2):
            ref[layer] = jnp.where(inside, ref[layer], 0.0)

    s, q = (s_own, s_halo, s_outer), (q_own, q_halo, q_outer)
    target, s1 = (target_own, target_halo), (s1_own, s1_halo)
    force, pull = (force_own, force_halo), (pull_own, pull_halo)
    for t in range(STEPS):
        model_step(s, q, target, s1, force, pull, inside, t, t == STEPS - 1)

    result = pltpu.make_async_copy(s_own, out.at[0], local_sem.at[0])
    result.start()
    result.wait()


def per_device(ensemble, offspring, new_owner, perturb, observed, nudge_rate):
    layers = pltpu.VMEM((2, ROWS, COLS), F32)
    forces = pltpu.VMEM((STEPS, 2, ROWS, COLS), F32)
    small = pltpu.VMEM((ROWS, LANES), F32)
    tiles = pltpu.VMEM((MEMBERS, 8, LANES), F32)
    dma = pltpu.SemaphoreType.DMA
    return pl.pallas_call(
        kernel,
        out_shape=jax.ShapeDtypeStruct(ensemble.shape, F32),
        in_specs=[pl.BlockSpec(memory_space=pltpu.HBM)] * 6,
        out_specs=pl.BlockSpec(memory_space=pltpu.HBM),
        scratch_shapes=[
            pltpu.SMEM((MEMBERS,), jnp.int32),
            pltpu.SMEM((MEMBERS,), jnp.int32),
            pltpu.SMEM((ROWS,), F32),
            pltpu.VMEM((STEPS, 2, ROWS, COLS), jnp.bfloat16),
            pltpu.VMEM((ROWS, COLS), F32),
            *[tiles] * 4,
            pltpu.VMEM((8, LANES), jnp.int32),
            pltpu.SMEM((8, LANES), jnp.int32),
            *[layers] * 10,
            forces,
            forces,
            small,
            small,
            dma((7,)),
            dma((2,)),
            dma((2,)),
            dma((2,)),
            dma((2, PLANES)),
            dma((6,)),
            dma((6,)),
            dma((4,)),
            dma((4,)),
        ],
        compiler_params=pltpu.CompilerParams(
            collective_id=0, has_side_effects=True, vmem_limit_bytes=60 * 1024 * 1024
        ),
        name="filter_step",
    )(offspring, new_owner, nudge_rate, ensemble, perturb, observed)


def solution(mesh):
    in_specs = (
        P("dom", None, "space", None),
        P(),
        P(),
        P("dom", None, None, "space", None),
        P("space", None),
        P("space"),
    )
    out_specs = P("dom", None, "space", None)
    return jax.shard_map(
        per_device, mesh=mesh, in_specs=in_specs, out_specs=out_specs, check_vma=False
    )
```

```python
import functools

import jax
import jax.numpy as jnp
from jax import lax
from jax.experimental import pallas as pl
from jax.experimental.pallas import tpu as pltpu
from jax.sharding import PartitionSpec as P

STEPS = 2
COLS = 4096
ROWS = 8
MEMBERS = 64
LANES = 128
PLANES = 8
PER_PLANE = 8
BAND = COLS // PLANES
PARTS = ((0, 4), (4, 4))
COUPLE = (0.4, 0.6)
DRAG = (0.0, 0.2)
DT = 0.05
BETA = 1.0
NOISE = 0.5
F32 = jnp.float32


def sublane(shape):
    return lax.broadcasted_iota(jnp.int32, shape, len(shape) - 2)


def west(value):
    return pltpu.roll(value, 1, 1)


def east(value):
    return pltpu.roll(value, COLS - 1, 1)


def up_of(value):
    return pltpu.roll(value, 1, 0)


def down_of(value):
    return pltpu.roll(value, ROWS - 1, 0)


def rows_beside(own, halo, outer):
    at = sublane(own.shape)
    up_o, up_h, down_o, down_h = up_of(own), up_of(halo), down_of(own), down_of(halo)
    above_o = jnp.where(at == 0, up_h, up_o)
    below_o = jnp.where(at == 7, down_h, down_o)
    above_h = jnp.where(at == 0, up_o, up_h)
    below_h = jnp.where(at == 7, down_o, down_h)
    if outer is None:
        return (above_o, above_h), (below_o, below_h)
    up_t, down_t = up_of(outer), down_of(outer)
    above_h = jnp.where(at == 4, up_t, above_h)
    below_h = jnp.where(at == 3, down_t, below_h)
    above_t = jnp.where(at == 4, up_h, up_t)
    below_t = jnp.where(at == 3, down_h, down_t)
    return (above_o, above_h, above_t), (below_o, below_h, below_t)


def laplace(value, above, below):
    return above + below + west(value) + east(value) - 4.0 * value


def model_step(s, q, target, s1, force, pull, inside, step_no, last, out):
    n_q = 2 if last else 3

    mine = [[s[i][layer] for i in range(n_q)] for layer in range(2)]
    for layer in range(2):
        above, below = rows_beside(*mine[layer], *[None] * (3 - n_q))
        for i in range(n_q):
            here, other = mine[layer][i], mine[1 - layer][i]
            value = laplace(here, above[i], below[i]) + COUPLE[layer] * (other - here)
            q[i][layer] = jnp.where(inside, value, 0.0) if i else value

    for layer in range(2):
        state, vort = [s[i][layer] for i in range(2)], [q[i][layer] for i in range(2)]
        s_above, s_below = rows_beside(*state, None if last else s[2][layer])
        q_above, q_below = rows_beside(*vort, None if last else q[2][layer])
        for i in range(2):
            ex_s = east(state[i]) - west(state[i])
            ex_q = east(vort[i]) - west(vort[i])
            ny_s = s_below[i] - s_above[i]
            ny_q = q_below[i] - q_above[i]
            tendency = (ny_s * ex_q - ex_s * ny_q) * 0.25 - (BETA * 0.5) * ex_s
            if DRAG[layer]:
                tendency = tendency - DRAG[layer] * vort[i]
            change = DT * tendency + force[i][step_no, layer]
            if layer == 0:
                change = change - pull[i][:, 0:1] * state[i]
            target[i][layer] = vort[i] + change
            value = state[i] - change * (1.0 / (4.0 + COUPLE[layer]))
            s1[i][layer] = jnp.where(inside, value, 0.0) if i else value

    mine = [[s1[i][layer] for i in range(2)] for layer in range(2)]
    for layer in range(2):
        above, below = rows_beside(*mine[layer], None)
        for i in range(1 if last else 2):
            here, other = mine[layer][i], mine[1 - layer][i]
            rest = (
                laplace(here, above[i], below[i])
                + COUPLE[layer] * (other - here)
                - target[i][layer]
            )
            value = here + rest * (1.0 / (4.0 + COUPLE[layer]))
            if last:
                out[0, layer] = value
            else:
                s[i][layer] = jnp.where(inside, value, 0.0) if i else value


def kernel(
    offspring_in, new_owner_in, nudge_in, ensemble, perturb, observed, out,
    offspring, new_owner, nudge, noise, obs, tiles_a, tiles_b, picked_a, picked_b,
    parent_row, parent_at,
    s_own, s_halo, s_outer, q_own, q_halo, q_outer, s1_own, s1_halo,
    target_own, target_halo, force_own, force_halo, pull_own, pull_halo,
    local_sem, spread_send, spread_recv, deliver_send, deliver_recv,
    early_send, early_recv, row_send, row_recv,
):
    me, x = lax.axis_index("dom"), lax.axis_index("space")
    next_x, prev_x = lax.rem(x + 1, 4), lax.rem(x + 3, 4)
    plane, y, core = lax.div(me, 8), lax.rem(lax.div(me, 2), 4), lax.rem(me, 2)
    tiles, picked = (tiles_a, tiles_b), (picked_a, picked_b)
    places = [
        (lax.rem(y + dy, 4) * 2 + lax.rem(core + dc, 2), lax.rem(y + dy, 4), lax.rem(core + dc, 2))
        for dy, dc in ((2, 1), (2, 0), (1, 1), (1, 0), (3, 1), (3, 0), (0, 1), (0, 0))
    ]

    def nth_plane(n):
        half = lax.div(n + 1, 2)
        return lax.rem(plane + jnp.where(lax.rem(n, 2) == 1, 4 - half, 4 + half), PLANES)

    def for_partners(act):
        def one_plane(n, carry, count=PER_PLANE):
            z = nth_plane(n)
            for place, at_y, at_core in places[:count]:
                act(z * PER_PLANE + place, at_core, pl.multiple_of((z * 4 + at_y) * LANES, LANES))
            return carry

        lax.fori_loop(0, PLANES - 1, one_plane, 0)
        one_plane(PLANES - 1, 0, PER_PLANE - 1)

    loads = [
        pltpu.make_async_copy(new_owner_in, new_owner, local_sem.at[0]),
        pltpu.make_async_copy(offspring_in, offspring, local_sem.at[1]),
        pltpu.make_async_copy(nudge_in, nudge, local_sem.at[2]),
        pltpu.make_async_copy(perturb.at[0], noise, local_sem.at[3]),
        pltpu.make_async_copy(observed, obs, local_sem.at[4]),
    ]
    for load in loads:
        load.start()

    barrier = pltpu.get_barrier_semaphore()
    for_partners(
        lambda to, layer, start: pl.semaphore_signal(barrier, inc=1, device_id=(to, x))
    )
    pl.semaphore_signal(barrier, inc=1, device_id=(me, next_x))
    pl.semaphore_signal(barrier, inc=1, device_id=(me, prev_x))
    pl.semaphore_wait(barrier, MEMBERS + 1)

    my_start = pl.multiple_of(lax.div(me, 2) * LANES, LANES)
    own_tiles = []
    for part, (row, count) in enumerate(PARTS):
        rows = pl.ds(row, count)

        def spread(to, layer, start, part=part, rows=rows):
            pltpu.make_async_remote_copy(
                src_ref=ensemble.at[0, layer, rows, pl.ds(start, LANES)],
                dst_ref=tiles[part].at[me, rows],
                send_sem=spread_send.at[part],
                recv_sem=spread_recv.at[part],
                device_id=(to, x),
            ).start()

        for_partners(spread)
        own = pltpu.make_async_copy(
            ensemble.at[0, core, rows, pl.ds(my_start, LANES)],
            tiles[part].at[me, rows],
            local_sem.at[5 + part],
        )
        own.start()
        own_tiles.append(own)

    for load in loads:
        load.wait()
    lane = lax.broadcasted_iota(jnp.int32, (8, LANES), 1)
    copy = jnp.zeros((8, LANES), jnp.int32)
    for j in range(MEMBERS):
        copy = jnp.where(lane == new_owner[j], j, copy)
    parent, total = jnp.zeros((8, LANES), jnp.int32), jnp.int32(0)
    for i in range(MEMBERS):
        total = total + offspring[i]
        parent = parent + (total <= copy).astype(jnp.int32)
    parent_row[...] = jnp.minimum(parent, MEMBERS - 1)
    to_scalars = pltpu.make_async_copy(parent_row, parent_at, local_sem.at[0])
    to_scalars.start()

    at = sublane((ROWS, LANES))
    rate = jnp.zeros((ROWS, LANES), F32)
    for r in range(ROWS):
        rate = jnp.where(at == r, DT * nudge[r], rate)
    pull_own[...] = rate
    drawn = rate[:, 0:1] * obs[...]
    for t in range(STEPS):
        for layer in range(2):
            value = NOISE * noise[t, layer].astype(F32)
            force_own[t, layer] = value + drawn if layer == 0 else value

    def early_copy(src, dst, number, to_x):
        return pltpu.make_async_remote_copy(
            src_ref=src,
            dst_ref=dst,
            send_sem=early_send.at[number],
            recv_sem=early_recv.at[number],
            device_id=(me, to_x),
        )

    low, high = pl.ds(0, 4), pl.ds(4, 4)
    early = [
        early_copy(force_own.at[0, :, low], force_halo.at[0, :, low], 0, prev_x),
        early_copy(force_own.at[0, :, high], force_halo.at[0, :, high], 1, next_x),
        early_copy(force_own.at[1, :, pl.ds(0, 1)], force_halo.at[1, :, pl.ds(0, 1)], 2, prev_x),
        early_copy(force_own.at[1, :, pl.ds(7, 1)], force_halo.at[1, :, pl.ds(7, 1)], 3, next_x),
        early_copy(pull_own.at[low], pull_halo.at[low], 4, prev_x),
        early_copy(pull_own.at[high], pull_halo.at[high], 5, next_x),
    ]
    for one in early:
        one.start()
    to_scalars.wait()

    def tiles_of(part, count):
        some = tiles[part].at[pl.ds(0, count), pl.ds(*PARTS[part])]
        return lambda sem: pltpu.make_async_copy(some, some, sem).wait()

    for part, (row, count) in enumerate(PARTS):
        rows = pl.ds(row, count)
        own_tiles[part].wait()
        tiles_of(part, MEMBERS - 1)(spread_recv.at[part])
        for m in range(MEMBERS):
            picked[part][m, rows] = tiles[part][parent_at[0, m], rows]

        def deliver(to, layer, start, part=part, rows=rows):
            pltpu.make_async_remote_copy(
                src_ref=picked[part].at[to, rows],
                dst_ref=s_own.at[core, rows, pl.ds(my_start, LANES)],
                send_sem=deliver_send.at[part],
                recv_sem=deliver_recv.at[part, plane],
                device_id=(to, x),
            ).start()

        for_partners(deliver)
        s_own[core, rows, pl.ds(my_start, LANES)] = picked[part][me, rows]

    def forward(part, z):
        band = pl.ds(pl.multiple_of(z * BAND, BAND), BAND)
        sides = (
            ((low, s_halo, prev_x, 0), (pl.ds(2, 2), s_outer, next_x, 1)),
            ((high, s_halo, next_x, 2), (pl.ds(4, 2), s_outer, prev_x, 3)),
        )[part]
        for rows, halo, to_x, number in sides:
            pltpu.make_async_remote_copy(
                src_ref=s_own.at[:, rows, band],
                dst_ref=halo.at[:, rows, band],
                send_sem=row_send.at[number],
                recv_sem=row_recv.at[number],
                device_id=(me, to_x),
            ).start()

    for part in range(len(PARTS)):

        def pass_on(n, carry, part=part, count=PER_PLANE):
            z = nth_plane(n)
            tiles_of(part, count)(deliver_recv.at[part, z])
            forward(part, z)
            return carry

        lax.fori_loop(0, PLANES - 1, pass_on, 0)
        pass_on(PLANES - 1, 0, count=PER_PLANE - 1)

    for part in range(len(PARTS)):
        tiles_of(part, MEMBERS - 1)(spread_send.at[part])
        tiles_of(part, MEMBERS - 1)(deliver_send.at[part])
    for one in early:
        one.wait()
    for number, count in enumerate((4, 2, 4, 2)):
        some = s_own.at[:, pl.ds(0, count)]
        for sem in (row_recv, row_send):
            pltpu.make_async_copy(some, some, sem.at[number]).wait()

    wide = sublane((ROWS, COLS))
    inside = jnp.where(wide < 4, jnp.where(x < 3, 1, 0), jnp.where(x > 0, 1, 0)) == 1
    for ref in (s_halo, s_outer):
        for layer in range(2):
            ref[layer] = jnp.where(inside, ref[layer], 0.0)

    s, q = (s_own, s_halo, s_outer), (q_own, q_halo, q_outer)
    target, s1 = (target_own, target_halo), (s1_own, s1_halo)
    force, pull = (force_own, force_halo), (pull_own, pull_halo)
    for t in range(STEPS):
        model_step(s, q, target, s1, force, pull, inside, t, t == STEPS - 1, out)


def per_device(ensemble, offspring, new_owner, perturb, observed, nudge_rate):
    layers = pltpu.VMEM((2, ROWS, COLS), F32)
    forces = pltpu.VMEM((STEPS, 2, ROWS, COLS), F32)
    small = pltpu.VMEM((ROWS, LANES), F32)
    tiles = pltpu.VMEM((MEMBERS, 8, LANES), F32)
    dma = pltpu.SemaphoreType.DMA
    operands = [
        pltpu.with_memory_space_constraint(a, pltpu.HBM)
        for a in (offspring, new_owner, nudge_rate, ensemble, perturb, observed)
    ]
    return pl.pallas_call(
        kernel,
        out_shape=pltpu.VMEM(ensemble.shape, F32),
        in_specs=[pl.BlockSpec(memory_space=pltpu.HBM)] * 6,
        out_specs=pl.BlockSpec(memory_space=pltpu.VMEM),
        scratch_shapes=[
            pltpu.SMEM((MEMBERS,), jnp.int32),
            pltpu.SMEM((MEMBERS,), jnp.int32),
            pltpu.SMEM((ROWS,), F32),
            pltpu.VMEM((STEPS, 2, ROWS, COLS), jnp.bfloat16),
            pltpu.VMEM((ROWS, COLS), F32),
            *[tiles] * 4,
            pltpu.VMEM((8, LANES), jnp.int32),
            pltpu.SMEM((8, LANES), jnp.int32),
            *[layers] * 10,
            forces,
            forces,
            small,
            small,
            dma((7,)),
            dma((2,)),
            dma((2,)),
            dma((2,)),
            dma((2, PLANES)),
            dma((6,)),
            dma((6,)),
            dma((4,)),
            dma((4,)),
        ],
        compiler_params=pltpu.CompilerParams(
            collective_id=0, has_side_effects=True, vmem_limit_bytes=48 * 1024 * 1024
        ),
        name="filter_step",
    )(*operands)


def solution(mesh):
    in_specs = (
        P("dom", None, "space", None),
        P(),
        P(),
        P("dom", None, None, "space", None),
        P("space", None),
        P("space"),
    )
    out_specs = P("dom", None, "space", None)
    return jax.shard_map(
        per_device, mesh=mesh, in_specs=in_specs, out_specs=out_specs, check_vma=False
    )
```

```python
import functools

import jax
import jax.numpy as jnp
from jax import lax
from jax.experimental import pallas as pl
from jax.experimental.pallas import tpu as pltpu
from jax.sharding import PartitionSpec as P

STEPS = 2
COLS = 4096
ROWS = 8
MEMBERS = 64
LANES = 128
PLANES = 8
PER_PLANE = 8
BAND = COLS // PLANES
PARTS = ((2, 2), (4, 2), (0, 2), (6, 2))
COUPLE = (0.4, 0.6)
DRAG = (0.0, 0.2)
DT = 0.05
BETA = 1.0
NOISE = 0.5
F32 = jnp.float32


def sublane(shape):
    return lax.broadcasted_iota(jnp.int32, shape, len(shape) - 2)


def west(value):
    return pltpu.roll(value, 1, 1)


def east(value):
    return pltpu.roll(value, COLS - 1, 1)


def up_of(value):
    return pltpu.roll(value, 1, 0)


def down_of(value):
    return pltpu.roll(value, ROWS - 1, 0)


def rows_beside(own, halo, outer):
    at = sublane(own.shape)
    up_o, up_h, down_o, down_h = up_of(own), up_of(halo), down_of(own), down_of(halo)
    above_o = jnp.where(at == 0, up_h, up_o)
    below_o = jnp.where(at == 7, down_h, down_o)
    above_h = jnp.where(at == 0, up_o, up_h)
    below_h = jnp.where(at == 7, down_o, down_h)
    if outer is None:
        return (above_o, above_h), (below_o, below_h)
    up_t, down_t = up_of(outer), down_of(outer)
    above_h = jnp.where(at == 4, up_t, above_h)
    below_h = jnp.where(at == 3, down_t, below_h)
    above_t = jnp.where(at == 4, up_h, up_t)
    below_t = jnp.where(at == 3, down_h, down_t)
    return (above_o, above_h, above_t), (below_o, below_h, below_t)


def laplace(value, above, below):
    return above + below + west(value) + east(value) - 4.0 * value


def model_step(s, q, target, s1, force, pull, inside, step_no, last, out):
    n_q = 2 if last else 3

    mine = [[s[i][layer] for i in range(n_q)] for layer in range(2)]
    for layer in range(2):
        above, below = rows_beside(*mine[layer], *[None] * (3 - n_q))
        for i in range(n_q):
            here, other = mine[layer][i], mine[1 - layer][i]
            value = laplace(here, above[i], below[i]) + COUPLE[layer] * (other - here)
            q[i][layer] = jnp.where(inside, value, 0.0) if i else value

    for layer in range(2):
        state, vort = [s[i][layer] for i in range(2)], [q[i][layer] for i in range(2)]
        s_above, s_below = rows_beside(*state, None if last else s[2][layer])
        q_above, q_below = rows_beside(*vort, None if last else q[2][layer])
        for i in range(2):
            ex_s = east(state[i]) - west(state[i])
            ex_q = east(vort[i]) - west(vort[i])
            ny_s = s_below[i] - s_above[i]
            ny_q = q_below[i] - q_above[i]
            tendency = (ny_s * ex_q - ex_s * ny_q) * 0.25 - (BETA * 0.5) * ex_s
            if DRAG[layer]:
                tendency = tendency - DRAG[layer] * vort[i]
            change = DT * tendency + force[i][step_no, layer]
            if layer == 0:
                change = change - pull[i][:, 0:1] * state[i]
            target[i][layer] = vort[i] + change
            value = state[i] - change * (1.0 / (4.0 + COUPLE[layer]))
            s1[i][layer] = jnp.where(inside, value, 0.0) if i else value

    mine = [[s1[i][layer] for i in range(2)] for layer in range(2)]
    for layer in range(2):
        above, below = rows_beside(*mine[layer], None)
        for i in range(1 if last else 2):
            here, other = mine[layer][i], mine[1 - layer][i]
            rest = (
                laplace(here, above[i], below[i])
                + COUPLE[layer] * (other - here)
                - target[i][layer]
            )
            value = here + rest * (1.0 / (4.0 + COUPLE[layer]))
            if last:
                out[0, layer] = value
            else:
                s[i][layer] = jnp.where(inside, value, 0.0) if i else value


def kernel(
    offspring_in, new_owner_in, nudge_in, ensemble, perturb, observed, out,
    offspring, new_owner, nudge, noise, obs, tiles, picked,
    parent_row, parent_at,
    s_own, s_halo, s_outer, q_own, q_halo, q_outer, s1_own, s1_halo,
    target_own, target_halo, force_own, force_halo, pull_own, pull_halo,
    local_sem, spread_send, spread_recv, deliver_send, deliver_recv,
    early_send, early_recv, row_send, row_recv,
):
    me, x = lax.axis_index("dom"), lax.axis_index("space")
    next_x, prev_x = lax.rem(x + 1, 4), lax.rem(x + 3, 4)
    plane, y, core = lax.div(me, 8), lax.rem(lax.div(me, 2), 4), lax.rem(me, 2)
    places = [
        (lax.rem(y + dy, 4) * 2 + lax.rem(core + dc, 2), lax.rem(y + dy, 4), lax.rem(core + dc, 2))
        for dy, dc in ((2, 1), (2, 0), (1, 1), (1, 0), (3, 1), (3, 0), (0, 1), (0, 0))
    ]

    def nth_plane(n):
        half = lax.div(n + 1, 2)
        return lax.rem(plane + jnp.where(lax.rem(n, 2) == 1, 4 - half, 4 + half), PLANES)

    def for_partners(act):
        def one_plane(n, carry, count=PER_PLANE):
            z = nth_plane(n)
            for place, at_y, at_core in places[:count]:
                act(z * PER_PLANE + place, at_core, pl.multiple_of((z * 4 + at_y) * LANES, LANES))
            return carry

        lax.fori_loop(0, PLANES - 1, one_plane, 0)
        one_plane(PLANES - 1, 0, PER_PLANE - 1)

    loads = [
        pltpu.make_async_copy(new_owner_in, new_owner, local_sem.at[0]),
        pltpu.make_async_copy(offspring_in, offspring, local_sem.at[1]),
        pltpu.make_async_copy(nudge_in, nudge, local_sem.at[2]),
        pltpu.make_async_copy(perturb.at[0], noise, local_sem.at[3]),
        pltpu.make_async_copy(observed, obs, local_sem.at[4]),
    ]
    for load in loads:
        load.start()

    barrier = pltpu.get_barrier_semaphore()
    for_partners(
        lambda to, layer, start: pl.semaphore_signal(barrier, inc=1, device_id=(to, x))
    )
    pl.semaphore_signal(barrier, inc=1, device_id=(me, next_x))
    pl.semaphore_signal(barrier, inc=1, device_id=(me, prev_x))
    pl.semaphore_wait(barrier, MEMBERS + 1)

    my_start = pl.multiple_of(lax.div(me, 2) * LANES, LANES)
    own_tiles = []
    for part, (row, count) in enumerate(PARTS):
        rows = pl.ds(row, count)

        def spread(to, layer, start, part=part, rows=rows):
            pltpu.make_async_remote_copy(
                src_ref=ensemble.at[0, layer, rows, pl.ds(start, LANES)],
                dst_ref=tiles[part].at[me, rows],
                send_sem=spread_send.at[part],
                recv_sem=spread_recv.at[part],
                device_id=(to, x),
            ).start()

        for_partners(spread)
        own = pltpu.make_async_copy(
            ensemble.at[0, core, rows, pl.ds(my_start, LANES)],
            tiles[part].at[me, rows],
            local_sem.at[5 + part],
        )
        own.start()
        own_tiles.append(own)

    for load in loads:
        load.wait()
    lane = lax.broadcasted_iota(jnp.int32, (8, LANES), 1)
    copy = jnp.zeros((8, LANES), jnp.int32)
    for j in range(MEMBERS):
        copy = jnp.where(lane == new_owner[j], j, copy)
    parent, total = jnp.zeros((8, LANES), jnp.int32), jnp.int32(0)
    for i in range(MEMBERS):
        total = total + offspring[i]
        parent = parent + (total <= copy).astype(jnp.int32)
    parent_row[...] = jnp.minimum(parent, MEMBERS - 1)
    to_scalars = pltpu.make_async_copy(parent_row, parent_at, local_sem.at[0])
    to_scalars.start()

    at = sublane((ROWS, LANES))
    rate = jnp.zeros((ROWS, LANES), F32)
    for r in range(ROWS):
        rate = jnp.where(at == r, DT * nudge[r], rate)
    pull_own[...] = rate
    drawn = rate[:, 0:1] * obs[...]
    for t in range(STEPS):
        for layer in range(2):
            value = NOISE * noise[t, layer].astype(F32)
            force_own[t, layer] = value + drawn if layer == 0 else value

    def early_copy(src, dst, number, to_x):
        return pltpu.make_async_remote_copy(
            src_ref=src,
            dst_ref=dst,
            send_sem=early_send.at[number],
            recv_sem=early_recv.at[number],
            device_id=(me, to_x),
        )

    low, high = pl.ds(0, 4), pl.ds(4, 4)
    early = [
        early_copy(force_own.at[0, :, low], force_halo.at[0, :, low], 0, prev_x),
        early_copy(force_own.at[0, :, high], force_halo.at[0, :, high], 1, next_x),
        early_copy(force_own.at[1, :, pl.ds(0, 1)], force_halo.at[1, :, pl.ds(0, 1)], 2, prev_x),
        early_copy(force_own.at[1, :, pl.ds(7, 1)], force_halo.at[1, :, pl.ds(7, 1)], 3, next_x),
        early_copy(pull_own.at[low], pull_halo.at[low], 4, prev_x),
        early_copy(pull_own.at[high], pull_halo.at[high], 5, next_x),
    ]
    for one in early:
        one.start()
    to_scalars.wait()

    def tiles_of(part, count):
        some = tiles[part].at[pl.ds(0, count), pl.ds(*PARTS[part])]
        return lambda sem: pltpu.make_async_copy(some, some, sem).wait()

    for part, (row, count) in enumerate(PARTS):
        rows = pl.ds(row, count)
        own_tiles[part].wait()
        tiles_of(part, MEMBERS - 1)(spread_recv.at[part])

        def one_plane(n, carry, part=part, rows=rows, count=PER_PLANE):
            z = nth_plane(n)
            for place in range(PER_PLANE):
                m = z * PER_PLANE + place
                picked[part][m, rows] = tiles[part][parent_at[0, m], rows]
            for place, _, _ in places[:count]:
                to = z * PER_PLANE + place
                pltpu.make_async_remote_copy(
                    src_ref=picked[part].at[to, rows],
                    dst_ref=s_own.at[core, rows, pl.ds(my_start, LANES)],
                    send_sem=deliver_send.at[part],
                    recv_sem=deliver_recv.at[part, plane],
                    device_id=(to, x),
                ).start()
            return carry

        lax.fori_loop(0, PLANES - 1, one_plane, 0)
        one_plane(PLANES - 1, 0, count=PER_PLANE - 1)
        s_own[core, rows, pl.ds(my_start, LANES)] = picked[part][me, rows]

    def forward(part, z):
        band = pl.ds(pl.multiple_of(z * BAND, BAND), BAND)
        row, count = PARTS[part]
        rows = pl.ds(row, count)
        sides = []
        if row < 6:
            sides.append((s_halo if row < 4 else s_outer, prev_x, 0))
        if row >= 2:
            sides.append((s_halo if row >= 4 else s_outer, next_x, 1))
        for halo, to_x, number in sides:
            pltpu.make_async_remote_copy(
                src_ref=s_own.at[:, rows, band],
                dst_ref=halo.at[:, rows, band],
                send_sem=row_send.at[number],
                recv_sem=row_recv.at[number],
                device_id=(me, to_x),
            ).start()

    for part in range(len(PARTS)):

        def pass_on(n, carry, part=part, count=PER_PLANE):
            z = nth_plane(n)
            tiles_of(part, count)(deliver_recv.at[part, z])
            forward(part, z)
            return carry

        lax.fori_loop(0, PLANES - 1, pass_on, 0)
        pass_on(PLANES - 1, 0, count=PER_PLANE - 1)

    for part in range(len(PARTS)):
        tiles_of(part, MEMBERS - 1)(spread_send.at[part])
        tiles_of(part, MEMBERS - 1)(deliver_send.at[part])
    for one in early:
        one.wait()
    for number in range(2):
        some = s_own.at[:, pl.ds(0, 6)]
        for sem in (row_recv, row_send):
            pltpu.make_async_copy(some, some, sem.at[number]).wait()

    wide = sublane((ROWS, COLS))
    inside = jnp.where(wide < 4, jnp.where(x < 3, 1, 0), jnp.where(x > 0, 1, 0)) == 1
    for ref in (s_halo, s_outer):
        for layer in range(2):
            ref[layer] = jnp.where(inside, ref[layer], 0.0)

    s, q = (s_own, s_halo, s_outer), (q_own, q_halo, q_outer)
    target, s1 = (target_own, target_halo), (s1_own, s1_halo)
    force, pull = (force_own, force_halo), (pull_own, pull_halo)
    for t in range(STEPS):
        model_step(s, q, target, s1, force, pull, inside, t, t == STEPS - 1, out)


def per_device(ensemble, offspring, new_owner, perturb, observed, nudge_rate):
    layers = pltpu.VMEM((2, ROWS, COLS), F32)
    forces = pltpu.VMEM((STEPS, 2, ROWS, COLS), F32)
    small = pltpu.VMEM((ROWS, LANES), F32)
    tiles = pltpu.VMEM((MEMBERS, 8, LANES), F32)
    dma = pltpu.SemaphoreType.DMA
    operands = [
        pltpu.with_memory_space_constraint(a, pltpu.HBM)
        for a in (offspring, new_owner, nudge_rate, ensemble, perturb, observed)
    ]
    return pl.pallas_call(
        kernel,
        out_shape=pltpu.VMEM(ensemble.shape, F32),
        in_specs=[pl.BlockSpec(memory_space=pltpu.HBM)] * 6,
        out_specs=pl.BlockSpec(memory_space=pltpu.VMEM),
        scratch_shapes=[
            pltpu.SMEM((MEMBERS,), jnp.int32),
            pltpu.SMEM((MEMBERS,), jnp.int32),
            pltpu.SMEM((ROWS,), F32),
            pltpu.VMEM((STEPS, 2, ROWS, COLS), jnp.bfloat16),
            pltpu.VMEM((ROWS, COLS), F32),
            [tiles] * len(PARTS),
            [tiles] * len(PARTS),
            pltpu.VMEM((8, LANES), jnp.int32),
            pltpu.SMEM((8, LANES), jnp.int32),
            *[layers] * 10,
            forces,
            forces,
            small,
            small,
            dma((5 + len(PARTS),)),
            dma((len(PARTS),)),
            dma((len(PARTS),)),
            dma((len(PARTS),)),
            dma((len(PARTS), PLANES)),
            dma((6,)),
            dma((6,)),
            dma((2,)),
            dma((2,)),
        ],
        compiler_params=pltpu.CompilerParams(
            collective_id=0, has_side_effects=True, vmem_limit_bytes=48 * 1024 * 1024
        ),
        name="filter_step",
    )(*operands)


def solution(mesh):
    in_specs = (
        P("dom", None, "space", None),
        P(),
        P(),
        P("dom", None, None, "space", None),
        P("space", None),
        P("space"),
    )
    out_specs = P("dom", None, "space", None)
    return jax.shard_map(
        per_device, mesh=mesh, in_specs=in_specs, out_specs=out_specs, check_vma=False
    )
```

```python
import jax
import jax.numpy as jnp
from jax import lax
from jax.experimental import pallas as pl
from jax.experimental.pallas import tpu as pltpu
from jax.sharding import PartitionSpec as P

STEPS = 2
COLS = 4096
ROWS = 8
SPACES = 4
MEMBERS = 64
LANES = 128
TILES = COLS // LANES
PLANES = 8
PER_PLANE = 8
BAND = TILES // PLANES
SPAN = 3 * ROWS
HALO = 6
SPREAD = ((2, 2), (4, 2), (0, 2), (6, 2))
DELIVER = (((2, 2),), ((4, 2),), ((0, 2),), ((6, 2),))
PARTS = [(spread, *rows) for spread, parts in enumerate(DELIVER) for rows in parts]
COUPLE = (0.4, 0.6)
DRAG = (0.0, 0.2)
DT = 0.05
BETA = 1.0
NOISE = 0.5
F32 = jnp.float32


def window(row, count=ROWS):
    return pl.ds(ROWS + row, count)


def shifted(ref, layer, row, by):
    turned = pltpu.roll(ref[layer, :, window(row), :], by % LANES, 2)
    lane = lax.broadcasted_iota(jnp.int32, turned.shape, 2)
    if by < 0:
        beside = jnp.concatenate([turned[1:], turned[:1]], axis=0)
        return jnp.where(lane == LANES - 1, beside, turned)
    beside = jnp.concatenate([turned[-1:], turned[:-1]], axis=0)
    return jnp.where(lane == 0, beside, turned)


def inside(x, row):
    if row == 0:
        return None
    at = lax.broadcasted_iota(jnp.int32, (TILES, ROWS, LANES), 1) + (x * ROWS + row)
    return (at >= 0) & (at < SPACES * ROWS)


def keep(value, mask):
    return value if mask is None else jnp.where(mask, value, 0.0)


def model_step(state, vort, slope, target, half, force, pull, x, step_no, last, out):
    for row in (-2, 2) if last else (-5, 3, 5):
        mask = inside(x, row)
        both = [state[layer, :, window(row), :] for layer in range(2)]
        for layer in range(2):
            left, right = shifted(state, layer, row, 1), shifted(state, layer, row, -1)
            above, below = (state[layer, :, window(row + by), :] for by in (-1, 1))
            value = (above + below) + (left + right) - (4.0 + COUPLE[layer]) * both[layer]
            value = value + COUPLE[layer] * both[1 - layer]
            vort[layer, :, window(row), :] = keep(value, mask)
            slope[layer, :, window(row), :] = right - left

    for row in (-1, 1) if last else (-4, 4):
        mask = inside(x, row)
        for layer in range(2):
            here, q = state[layer, :, window(row), :], vort[layer, :, window(row), :]
            ex_s = slope[layer, :, window(row), :]
            ex_q = shifted(vort, layer, row, -1) - shifted(vort, layer, row, 1)
            ny_s = state[layer, :, window(row + 1), :] - state[layer, :, window(row - 1), :]
            ny_q = vort[layer, :, window(row + 1), :] - vort[layer, :, window(row - 1), :]
            tendency = ny_s * ex_q - ex_s * (ny_q + 2.0 * BETA)
            change = (DT * 0.25) * tendency + force[step_no, layer, :, window(row), :]
            if DRAG[layer]:
                change = change - (DT * DRAG[layer]) * q
            if layer == 0:
                change = change - pull[window(row), :] * here
            target[layer, :, window(row), :] = q + change
            value = here - change * (1.0 / (4.0 + COUPLE[layer]))
            half[layer, :, window(row), :] = keep(value, mask)

    for row in (0,) if last else (-3, 3):
        mask = inside(x, row)
        both = [half[layer, :, window(row), :] for layer in range(2)]
        for layer in range(2):
            around = half[layer, :, window(row - 1), :] + half[layer, :, window(row + 1), :]
            around = around + shifted(half, layer, row, 1) + shifted(half, layer, row, -1)
            rest = around + COUPLE[layer] * both[1 - layer] - target[layer, :, window(row), :]
            value = rest * (1.0 / (4.0 + COUPLE[layer]))
            if last:
                for tile in range(TILES):
                    out[0, layer, :, pl.ds(tile * LANES, LANES)] = value[tile]
            else:
                state[layer, :, window(row), :] = keep(value, mask)


def kernel(
    offspring_in, new_owner_in, nudge_in, ensemble, perturb, observed, out,
    offspring, new_owner, nudge, noise, obs, tiles, picked, parent_row, parent_at,
    state, vort, slope, target, half, force, pull,
    local_sem, spread_send, spread_recv, deliver_send, deliver_recv,
    early_send, early_recv, row_send, row_recv,
):
    me, x = lax.axis_index("dom"), lax.axis_index("space")
    plane, y, core = lax.div(me, 8), lax.rem(lax.div(me, 2), 4), lax.rem(me, 2)
    my_tile = lax.div(me, 2)
    places = [
        (lax.rem(y + dy, 4), lax.rem(core + dc, 2))
        for dy, dc in ((2, 1), (2, 0), (1, 1), (1, 0), (3, 1), (3, 0), (0, 1), (0, 0))
    ]

    def nth_plane(n):
        far = (n + 1) // 2
        return lax.rem(plane + jnp.where(n % 2 == 1, 4 - far, 4 + far), PLANES)

    def each_plane(act):
        def one_plane(n, carry):
            act(nth_plane(n), PER_PLANE)
            return carry

        lax.fori_loop(0, PLANES - 1, one_plane, 0)
        act(plane, PER_PLANE - 1)

    def each_partner(act):
        def in_plane(z, count):
            for at_y, at_core in places[:count]:
                act(z * PER_PLANE + at_y * 2 + at_core, z, at_y, at_core)

        each_plane(in_plane)

    loads = [
        pltpu.make_async_copy(new_owner_in, new_owner, local_sem.at[0]),
        pltpu.make_async_copy(offspring_in, offspring, local_sem.at[1]),
        pltpu.make_async_copy(nudge_in, nudge, local_sem.at[2]),
        pltpu.make_async_copy(perturb.at[0], noise, local_sem.at[3]),
        pltpu.make_async_copy(observed, obs, local_sem.at[4]),
    ]
    for load in loads:
        load.start()

    barrier = pltpu.get_barrier_semaphore()
    each_partner(lambda to, *_: pl.semaphore_signal(barrier, inc=1, device_id=(to, x)))

    has_prev, has_next = x > 0, x < SPACES - 1

    @pl.when(has_prev)
    def _():
        pl.semaphore_signal(barrier, inc=1, device_id=(me, x - 1))

    @pl.when(has_next)
    def _():
        pl.semaphore_signal(barrier, inc=1, device_id=(me, x + 1))

    beside = jnp.where(has_prev, 1, 0) + jnp.where(has_next, 1, 0)
    pl.semaphore_wait(barrier, MEMBERS - 1 + beside)

    own_tiles = []
    for part, (row, count) in enumerate(SPREAD):
        rows = pl.ds(row, count)

        def spread_to(to, z, at_y, at_core, part=part, rows=rows):
            start = pl.multiple_of((z * 4 + at_y) * LANES, LANES)
            pltpu.make_async_remote_copy(
                src_ref=ensemble.at[0, at_core, rows, pl.ds(start, LANES)],
                dst_ref=tiles[part].at[me, rows],
                send_sem=spread_send.at[part],
                recv_sem=spread_recv.at[part],
                device_id=(to, x),
            ).start()

        each_partner(spread_to)
        start = pl.multiple_of(my_tile * LANES, LANES)
        own = pltpu.make_async_copy(
            ensemble.at[0, core, rows, pl.ds(start, LANES)],
            tiles[part].at[me, rows],
            local_sem.at[5 + part],
        )
        own.start()
        own_tiles.append(own)

    for load in loads:
        load.wait()
    lane = lax.broadcasted_iota(jnp.int32, (8, LANES), 1)
    copy = jnp.zeros((8, LANES), jnp.int32)
    for j in range(MEMBERS):
        copy = jnp.where(lane == new_owner[j], j, copy)
    parent, total = jnp.zeros((8, LANES), jnp.int32), jnp.int32(0)
    for i in range(MEMBERS):
        total = total + offspring[i]
        parent = parent + (total <= copy).astype(jnp.int32)
    parent_row[...] = jnp.minimum(parent, MEMBERS - 1)
    to_scalars = pltpu.make_async_copy(parent_row, parent_at, local_sem.at[0])
    to_scalars.start()

    at = lax.broadcasted_iota(jnp.int32, (ROWS, LANES), 0)
    rate = jnp.zeros((ROWS, LANES), F32)
    for r in range(ROWS):
        rate = jnp.where(at == r, DT * nudge[r], rate)
    own_rows = window(0)
    pull[own_rows, :] = rate
    for tile in range(TILES):
        here = pl.ds(tile * LANES, LANES)
        drawn = rate * obs[:, here]
        for t in range(STEPS):
            for layer in range(2):
                value = NOISE * noise[t, layer, :, here].astype(F32)
                force[t, layer, tile, own_rows, :] = value + drawn if layer == 0 else value

    def row_copy(src, dst, send, recv, to_x):
        return pltpu.make_async_remote_copy(
            src_ref=src, dst_ref=dst, send_sem=send, recv_sem=recv, device_id=(me, to_x)
        )

    def early_copies(side):
        copies = []
        by, to_x = ((ROWS, x - 1), (-ROWS, x + 1))[side]
        for number, (row, count) in enumerate((((0, 4), (0, 1)), ((4, 4), (7, 1)))[side]):
            src, dst = window(row, count), window(row + by, count)
            copies.append((force.at[number, :, :, src, :], force.at[number, :, :, dst, :]))
            if number == 0:
                copies.append((pull.at[src, :], pull.at[dst, :]))
        return [
            row_copy(src, dst, early_send.at[side, n], early_recv.at[side, n], to_x)
            for n, (src, dst) in enumerate(copies)
        ]

    @pl.when(has_prev)
    def _():
        for one in early_copies(0):
            one.start()

    @pl.when(has_next)
    def _():
        for one in early_copies(1):
            one.start()

    to_scalars.wait()

    def tiles_of(row, count, number):
        some = tiles[0].at[pl.ds(0, number), pl.ds(row, count)]
        return lambda sem: pltpu.make_async_copy(some, some, sem).wait()

    arrived = -1
    for part, (spread, row, count) in enumerate(PARTS):
        if spread > arrived:
            arrived = spread
            own_tiles[spread].wait()
            tiles_of(*SPREAD[spread], MEMBERS - 1)(spread_recv.at[spread])
        rows, lands = pl.ds(row, count), window(row, count)

        def deliver_in(z, count, part=part, spread=spread, rows=rows, lands=lands):
            for place in range(PER_PLANE):
                m = z * PER_PLANE + place
                picked[part][m, rows] = tiles[spread][parent_at[0, m], rows]
            for at_y, at_core in places[:count]:
                to = z * PER_PLANE + at_y * 2 + at_core
                pltpu.make_async_remote_copy(
                    src_ref=picked[part].at[to, rows],
                    dst_ref=state.at[core, my_tile, lands, :],
                    send_sem=deliver_send.at[part],
                    recv_sem=deliver_recv.at[part, plane],
                    device_id=(to, x),
                ).start()

        each_plane(deliver_in)
        state[core, my_tile, lands, :] = picked[part][me, rows]

    for part, (_, row, count) in enumerate(PARTS):

        def pass_on(z, number, part=part, row=row, count=count):
            tiles_of(row, count, number)(deliver_recv.at[part, z])
            band = pl.ds(z * BAND, BAND)
            for side, (by, to_x, there) in enumerate(
                ((ROWS, x - 1, has_prev), (-ROWS, x + 1, has_next))
            ):
                if row < HALO if side == 0 else row >= ROWS - HALO:

                    @pl.when(there)
                    def _(side=side, by=by, to_x=to_x):
                        row_copy(
                            state.at[:, band, window(row, count), :],
                            state.at[:, band, window(row + by, count), :],
                            row_send.at[side],
                            row_recv.at[side],
                            to_x,
                        ).start()

        each_plane(pass_on)

    for part, rows in enumerate(SPREAD):
        tiles_of(*rows, MEMBERS - 1)(spread_send.at[part])
    for part, (_, *rows) in enumerate(PARTS):
        tiles_of(*rows, MEMBERS - 1)(deliver_send.at[part])

    some = state.at[:, :, window(0, HALO), :]
    for side, (there, row) in enumerate(((has_prev, -HALO), (has_next, ROWS))):

        @pl.when(there)
        def _(side=side):
            for one in early_copies(side):
                one.wait_send()
            for one in early_copies(1 - side):
                one.wait_recv()
            pltpu.make_async_copy(some, some, row_send.at[side]).wait()
            pltpu.make_async_copy(some, some, row_recv.at[1 - side]).wait()

        @pl.when(jnp.logical_not(there))
        def _(row=row):
            state[:, :, window(row, HALO), :] = jnp.zeros((2, TILES, HALO, LANES), F32)

    for t in range(STEPS):
        model_step(state, vort, slope, target, half, force, pull, x, t, t == STEPS - 1, out)


def per_device(ensemble, offspring, new_owner, perturb, observed, nudge_rate):
    field = pltpu.VMEM((2, TILES, SPAN, LANES), F32)
    tiles = pltpu.VMEM((MEMBERS, 8, LANES), F32)
    dma = pltpu.SemaphoreType.DMA
    operands = [
        pltpu.with_memory_space_constraint(a, pltpu.HBM)
        for a in (offspring, new_owner, nudge_rate, ensemble, perturb, observed)
    ]
    return pl.pallas_call(
        kernel,
        out_shape=pltpu.VMEM(ensemble.shape, F32),
        in_specs=[pl.BlockSpec(memory_space=pltpu.HBM)] * 6,
        out_specs=pl.BlockSpec(memory_space=pltpu.VMEM),
        scratch_shapes=[
            pltpu.SMEM((MEMBERS,), jnp.int32),
            pltpu.SMEM((MEMBERS,), jnp.int32),
            pltpu.SMEM((ROWS,), F32),
            pltpu.VMEM((STEPS, 2, ROWS, COLS), jnp.bfloat16),
            pltpu.VMEM((ROWS, COLS), F32),
            [tiles] * len(SPREAD),
            [tiles] * len(PARTS),
            pltpu.VMEM((8, LANES), jnp.int32),
            pltpu.SMEM((8, LANES), jnp.int32),
            *[field] * 5,
            pltpu.VMEM((STEPS, 2, TILES, SPAN, LANES), F32),
            pltpu.VMEM((SPAN, LANES), F32),
            dma((5 + len(SPREAD),)),
            dma((len(SPREAD),)),
            dma((len(SPREAD),)),
            dma((len(PARTS),)),
            dma((len(PARTS), PLANES)),
            dma((2, 3)),
            dma((2, 3)),
            dma((2,)),
            dma((2,)),
        ],
        compiler_params=pltpu.CompilerParams(
            collective_id=0, has_side_effects=True, vmem_limit_bytes=48 * 1024 * 1024
        ),
        name="filter_step",
    )(*operands)


def solution(mesh):
    in_specs = (
        P("dom", None, "space", None),
        P(),
        P(),
        P("dom", None, None, "space", None),
        P("space", None),
        P("space"),
    )
    out_specs = P("dom", None, "space", None)
    return jax.shard_map(
        per_device, mesh=mesh, in_specs=in_specs, out_specs=out_specs, check_vma=False
    )
```

```python
import jax
import jax.numpy as jnp
from jax import lax
from jax.experimental import pallas as pl
from jax.experimental.pallas import tpu as pltpu
from jax.sharding import PartitionSpec as P

STEPS = 2
COLS = 4096
ROWS = 8
SPACES = 4
MEMBERS = 64
LANES = 128
TILES = COLS // LANES
PLANES = 8
PER_PLANE = 8
BAND = TILES // PLANES
SPAN = 3 * ROWS
HALO = 6
SPREAD = ((2, 2), (4, 2), (0, 2), (6, 2))
DELIVER = (((2, 2),), ((4, 2),), ((0, 2),), ((6, 2),))
PARTS = [(spread, *rows) for spread, parts in enumerate(DELIVER) for rows in parts]
DIRECT = (2, 3)
COUPLE = (0.4, 0.6)
DRAG = (0.0, 0.2)
DT = 0.05
BETA = 1.0
NOISE = 0.5
F32 = jnp.float32


def window(row, count=ROWS):
    return pl.ds(ROWS + row, count)


def shifted(ref, layer, row, by):
    turned = pltpu.roll(ref[layer, :, window(row), :], by % LANES, 2)
    lane = lax.broadcasted_iota(jnp.int32, turned.shape, 2)
    if by < 0:
        beside = jnp.concatenate([turned[1:], turned[:1]], axis=0)
        return jnp.where(lane == LANES - 1, beside, turned)
    beside = jnp.concatenate([turned[-1:], turned[:-1]], axis=0)
    return jnp.where(lane == 0, beside, turned)


def inside(x, row):
    if row == 0:
        return None
    at = lax.broadcasted_iota(jnp.int32, (TILES, ROWS, LANES), 1) + (x * ROWS + row)
    return (at >= 0) & (at < SPACES * ROWS)


def keep(value, mask):
    return value if mask is None else jnp.where(mask, value, 0.0)


def model_step(state, vort, slope, target, half, force, pull, x, step_no, last, out):
    for row in (-2, 2) if last else (-5, 3, 5):
        mask = inside(x, row)
        both = [state[layer, :, window(row), :] for layer in range(2)]
        for layer in range(2):
            left, right = shifted(state, layer, row, 1), shifted(state, layer, row, -1)
            above, below = (state[layer, :, window(row + by), :] for by in (-1, 1))
            value = (above + below) + (left + right) - (4.0 + COUPLE[layer]) * both[layer]
            value = value + COUPLE[layer] * both[1 - layer]
            vort[layer, :, window(row), :] = keep(value, mask)
            slope[layer, :, window(row), :] = right - left

    for row in (-1, 1) if last else (-4, 4):
        mask = inside(x, row)
        for layer in range(2):
            here, q = state[layer, :, window(row), :], vort[layer, :, window(row), :]
            ex_s = slope[layer, :, window(row), :]
            ex_q = shifted(vort, layer, row, -1) - shifted(vort, layer, row, 1)
            ny_s = state[layer, :, window(row + 1), :] - state[layer, :, window(row - 1), :]
            ny_q = vort[layer, :, window(row + 1), :] - vort[layer, :, window(row - 1), :]
            tendency = ny_s * ex_q - ex_s * (ny_q + 2.0 * BETA)
            change = (DT * 0.25) * tendency + force[step_no, layer, :, window(row), :]
            if DRAG[layer]:
                change = change - (DT * DRAG[layer]) * q
            if layer == 0:
                change = change - pull[window(row), :] * here
            target[layer, :, window(row), :] = q + change
            value = here - change * (1.0 / (4.0 + COUPLE[layer]))
            half[layer, :, window(row), :] = keep(value, mask)

    for row in (0,) if last else (-3, 3):
        mask = inside(x, row)
        both = [half[layer, :, window(row), :] for layer in range(2)]
        for layer in range(2):
            around = half[layer, :, window(row - 1), :] + half[layer, :, window(row + 1), :]
            around = around + shifted(half, layer, row, 1) + shifted(half, layer, row, -1)
            rest = around + COUPLE[layer] * both[1 - layer] - target[layer, :, window(row), :]
            value = rest * (1.0 / (4.0 + COUPLE[layer]))
            if last:
                for tile in range(TILES):
                    out[0, layer, :, pl.ds(tile * LANES, LANES)] = value[tile]
            else:
                state[layer, :, window(row), :] = keep(value, mask)


def kernel(
    offspring_in, new_owner_in, nudge_in, ensemble, perturb, observed, out,
    offspring, new_owner, nudge, noise, obs, tiles, picked, parent_row, parent_at,
    state, vort, slope, target, half, force, pull,
    local_sem, spread_send, spread_recv, deliver_send, deliver_recv,
    early_send, early_recv, row_send, row_recv, direct_send, direct_recv,
):
    me, x = lax.axis_index("dom"), lax.axis_index("space")
    plane, y, core = lax.div(me, 8), lax.rem(lax.div(me, 2), 4), lax.rem(me, 2)
    my_tile = lax.div(me, 2)
    places = [
        (lax.rem(y + dy, 4), lax.rem(core + dc, 2))
        for dy, dc in ((2, 1), (2, 0), (1, 1), (1, 0), (3, 1), (3, 0), (0, 1), (0, 0))
    ]

    def nth_plane(n):
        far = (n + 1) // 2
        return lax.rem(plane + jnp.where(n % 2 == 1, 4 - far, 4 + far), PLANES)

    def each_plane(act):
        def one_plane(n, carry):
            act(nth_plane(n), PER_PLANE)
            return carry

        lax.fori_loop(0, PLANES - 1, one_plane, 0)
        act(plane, PER_PLANE - 1)

    def each_partner(act):
        def in_plane(z, count):
            for at_y, at_core in places[:count]:
                act(z * PER_PLANE + at_y * 2 + at_core, z, at_y, at_core)

        each_plane(in_plane)

    loads = [
        pltpu.make_async_copy(new_owner_in, new_owner, local_sem.at[0]),
        pltpu.make_async_copy(offspring_in, offspring, local_sem.at[1]),
        pltpu.make_async_copy(nudge_in, nudge, local_sem.at[2]),
        pltpu.make_async_copy(perturb.at[0], noise, local_sem.at[3]),
        pltpu.make_async_copy(observed, obs, local_sem.at[4]),
    ]
    for load in loads:
        load.start()

    barrier = pltpu.get_barrier_semaphore()
    each_partner(lambda to, *_: pl.semaphore_signal(barrier, inc=1, device_id=(to, x)))

    has_prev, has_next = x > 0, x < SPACES - 1

    @pl.when(has_prev)
    def _():
        pl.semaphore_signal(barrier, inc=1, device_id=(me, x - 1))

    @pl.when(has_next)
    def _():
        pl.semaphore_signal(barrier, inc=1, device_id=(me, x + 1))

    beside = jnp.where(has_prev, 1, 0) + jnp.where(has_next, 1, 0)
    pl.semaphore_wait(barrier, MEMBERS - 1 + beside)

    own_tiles = []
    for part, (row, count) in enumerate(SPREAD):
        rows = pl.ds(row, count)

        def spread_to(to, z, at_y, at_core, part=part, rows=rows):
            start = pl.multiple_of((z * 4 + at_y) * LANES, LANES)
            pltpu.make_async_remote_copy(
                src_ref=ensemble.at[0, at_core, rows, pl.ds(start, LANES)],
                dst_ref=tiles[part].at[me, rows],
                send_sem=spread_send.at[part],
                recv_sem=spread_recv.at[part],
                device_id=(to, x),
            ).start()

        each_partner(spread_to)
        start = pl.multiple_of(my_tile * LANES, LANES)
        own = pltpu.make_async_copy(
            ensemble.at[0, core, rows, pl.ds(start, LANES)],
            tiles[part].at[me, rows],
            local_sem.at[5 + part],
        )
        own.start()
        own_tiles.append(own)

    for load in loads:
        load.wait()
    lane = lax.broadcasted_iota(jnp.int32, (8, LANES), 1)
    copy = jnp.zeros((8, LANES), jnp.int32)
    for j in range(MEMBERS):
        copy = jnp.where(lane == new_owner[j], j, copy)
    parent, total = jnp.zeros((8, LANES), jnp.int32), jnp.int32(0)
    for i in range(MEMBERS):
        total = total + offspring[i]
        parent = parent + (total <= copy).astype(jnp.int32)
    parent_row[...] = jnp.minimum(parent, MEMBERS - 1)
    to_scalars = pltpu.make_async_copy(parent_row, parent_at, local_sem.at[0])
    to_scalars.start()

    at = lax.broadcasted_iota(jnp.int32, (ROWS, LANES), 0)
    rate = jnp.zeros((ROWS, LANES), F32)
    for r in range(ROWS):
        rate = jnp.where(at == r, DT * nudge[r], rate)
    own_rows = window(0)
    pull[own_rows, :] = rate
    for tile in range(TILES):
        here = pl.ds(tile * LANES, LANES)
        drawn = rate * obs[:, here]
        for t in range(STEPS):
            for layer in range(2):
                value = NOISE * noise[t, layer, :, here].astype(F32)
                force[t, layer, tile, own_rows, :] = value + drawn if layer == 0 else value

    def row_copy(src, dst, send, recv, to_x):
        return pltpu.make_async_remote_copy(
            src_ref=src, dst_ref=dst, send_sem=send, recv_sem=recv, device_id=(me, to_x)
        )

    def early_copies(side):
        copies = []
        by, to_x = ((ROWS, x - 1), (-ROWS, x + 1))[side]
        for number, (row, count) in enumerate((((0, 4), (0, 1)), ((4, 4), (7, 1)))[side]):
            src, dst = window(row, count), window(row + by, count)
            copies.append((force.at[number, :, :, src, :], force.at[number, :, :, dst, :]))
            if number == 0:
                copies.append((pull.at[src, :], pull.at[dst, :]))
        return [
            row_copy(src, dst, early_send.at[side, n], early_recv.at[side, n], to_x)
            for n, (src, dst) in enumerate(copies)
        ]

    @pl.when(has_prev)
    def _():
        for one in early_copies(0):
            one.start()

    @pl.when(has_next)
    def _():
        for one in early_copies(1):
            one.start()

    to_scalars.wait()

    def tiles_of(row, count, number):
        some = tiles[0].at[pl.ds(0, number), pl.ds(row, count)]
        return lambda sem: pltpu.make_async_copy(some, some, sem).wait()

    def sides_of(row):
        sides = ((0, (ROWS, x - 1, has_prev)), (1, (-ROWS, x + 1, has_next)))
        return [sides[n] for n in (0, 1) if (row >= ROWS - HALO if n else row < HALO)]

    arrived = -1
    for part, (spread, row, count) in enumerate(PARTS):
        if spread > arrived:
            arrived = spread
            own_tiles[spread].wait()
            tiles_of(*SPREAD[spread], MEMBERS - 1)(spread_recv.at[spread])
        rows, lands = pl.ds(row, count), window(row, count)

        def deliver_in(
            z, count, part=part, spread=spread, row=row, size=count, rows=rows, lands=lands
        ):
            for place in range(PER_PLANE):
                m = z * PER_PLANE + place
                picked[part][m, rows] = tiles[spread][parent_at[0, m], rows]
            for at_y, at_core in places[:count]:
                to = z * PER_PLANE + at_y * 2 + at_core
                pltpu.make_async_remote_copy(
                    src_ref=picked[part].at[to, rows],
                    dst_ref=state.at[core, my_tile, lands, :],
                    send_sem=deliver_send.at[part],
                    recv_sem=deliver_recv.at[part, plane],
                    device_id=(to, x),
                ).start()
            if part in DIRECT:
                for side, (by, to_x, there) in sides_of(row):

                    @pl.when(there)
                    def _(side=side, by=by, to_x=to_x):
                        for at_y, at_core in places:
                            to = z * PER_PLANE + at_y * 2 + at_core
                            pltpu.make_async_remote_copy(
                                src_ref=picked[part].at[to, rows],
                                dst_ref=state.at[core, my_tile, window(row + by, size), :],
                                send_sem=direct_send.at[part],
                                recv_sem=direct_recv.at[part],
                                device_id=(to, to_x),
                            ).start()

        each_plane(deliver_in)
        state[core, my_tile, lands, :] = picked[part][me, rows]

    for part, (_, row, count) in enumerate(PARTS):

        def pass_on(z, number, part=part, row=row, count=count):
            tiles_of(row, count, number)(deliver_recv.at[part, z])
            band = pl.ds(z * BAND, BAND)
            for side, (by, to_x, there) in sides_of(row):
                if part not in DIRECT:

                    @pl.when(there)
                    def _(side=side, by=by, to_x=to_x):
                        row_copy(
                            state.at[:, band, window(row, count), :],
                            state.at[:, band, window(row + by, count), :],
                            row_send.at[side],
                            row_recv.at[side],
                            to_x,
                        ).start()

        each_plane(pass_on)

    for part, rows in enumerate(SPREAD):
        tiles_of(*rows, MEMBERS - 1)(spread_send.at[part])
    for part, (_, *rows) in enumerate(PARTS):
        tiles_of(*rows, MEMBERS - 1)(deliver_send.at[part])

    passed = [
        sum(n for part, (_, r, n) in enumerate(PARTS) if part not in DIRECT and (r >= ROWS - HALO if side else r < HALO))
        for side in (0, 1)
    ]
    for side, (there, row) in enumerate(((has_prev, -HALO), (has_next, ROWS))):

        @pl.when(there)
        def _(side=side):
            for one in early_copies(side):
                one.wait_send()
            for one in early_copies(1 - side):
                one.wait_recv()
            gone = state.at[:, :, window(0, passed[side]), :]
            came = state.at[:, :, window(0, passed[1 - side]), :]
            pltpu.make_async_copy(gone, gone, row_send.at[side]).wait()
            pltpu.make_async_copy(came, came, row_recv.at[1 - side]).wait()
            for part in DIRECT:
                _, row, count = PARTS[part]
                if side in [n for n, _ in sides_of(row)]:
                    tiles_of(row, count, MEMBERS)(direct_send.at[part])
                else:
                    tiles_of(row, count, MEMBERS)(direct_recv.at[part])

        @pl.when(jnp.logical_not(there))
        def _(row=row):
            state[:, :, window(row, HALO), :] = jnp.zeros((2, TILES, HALO, LANES), F32)

    for t in range(STEPS):
        model_step(state, vort, slope, target, half, force, pull, x, t, t == STEPS - 1, out)


def per_device(ensemble, offspring, new_owner, perturb, observed, nudge_rate):
    field = pltpu.VMEM((2, TILES, SPAN, LANES), F32)
    tiles = pltpu.VMEM((MEMBERS, 8, LANES), F32)
    dma = pltpu.SemaphoreType.DMA
    operands = [
        pltpu.with_memory_space_constraint(a, pltpu.HBM)
        for a in (offspring, new_owner, nudge_rate, ensemble, perturb, observed)
    ]
    return pl.pallas_call(
        kernel,
        out_shape=pltpu.VMEM(ensemble.shape, F32),
        in_specs=[pl.BlockSpec(memory_space=pltpu.HBM)] * 6,
        out_specs=pl.BlockSpec(memory_space=pltpu.VMEM),
        scratch_shapes=[
            pltpu.SMEM((MEMBERS,), jnp.int32),
            pltpu.SMEM((MEMBERS,), jnp.int32),
            pltpu.SMEM((ROWS,), F32),
            pltpu.VMEM((STEPS, 2, ROWS, COLS), jnp.bfloat16),
            pltpu.VMEM((ROWS, COLS), F32),
            [tiles] * len(SPREAD),
            [tiles] * len(PARTS),
            pltpu.VMEM((8, LANES), jnp.int32),
            pltpu.SMEM((8, LANES), jnp.int32),
            *[field] * 5,
            pltpu.VMEM((STEPS, 2, TILES, SPAN, LANES), F32),
            pltpu.VMEM((SPAN, LANES), F32),
            dma((5 + len(SPREAD),)),
            dma((len(SPREAD),)),
            dma((len(SPREAD),)),
            dma((len(PARTS),)),
            dma((len(PARTS), PLANES)),
            dma((2, 3)),
            dma((2, 3)),
            dma((2,)),
            dma((2,)),
            dma((len(PARTS),)),
            dma((len(PARTS),)),
        ],
        compiler_params=pltpu.CompilerParams(
            collective_id=0, has_side_effects=True, vmem_limit_bytes=48 * 1024 * 1024
        ),
        name="filter_step",
    )(*operands)


def solution(mesh):
    in_specs = (
        P("dom", None, "space", None),
        P(),
        P(),
        P("dom", None, None, "space", None),
        P("space", None),
        P("space"),
    )
    out_specs = P("dom", None, "space", None)
    return jax.shard_map(
        per_device, mesh=mesh, in_specs=in_specs, out_specs=out_specs, check_vma=False
    )
```

```python
import jax
import jax.numpy as jnp
from jax import lax
from jax.experimental import pallas as pl
from jax.experimental.pallas import tpu as pltpu
from jax.sharding import PartitionSpec as P

STEPS = 2
COLS = 4096
ROWS = 8
SPACES = 4
MEMBERS = 64
LANES = 128
TILES = COLS // LANES
PLANES = 8
PER_PLANE = 8
BAND = TILES // PLANES
SPAN = 3 * ROWS
HALO = 6
SPREAD = ((2, 2), (4, 2), (0, 2), (6, 2))
DELIVER = (((2, 2),), ((4, 2),), ((0, 2),), ((6, 2),))
PARTS = [(spread, *rows) for spread, parts in enumerate(DELIVER) for rows in parts]
DIRECT = (2, 3)
COUPLE = (0.4, 0.6)
DRAG = (0.0, 0.2)
DT = 0.05
BETA = 1.0
NOISE = 0.5
F32 = jnp.float32


def window(row, count=ROWS):
    return pl.ds(ROWS + row, count)


def shifted(ref, layer, row, by, count=ROWS):
    turned = pltpu.roll(ref[layer, :, window(row, count), :], by % LANES, 2)
    lane = lax.broadcasted_iota(jnp.int32, turned.shape, 2)
    if by < 0:
        beside = jnp.concatenate([turned[1:], turned[:1]], axis=0)
        return jnp.where(lane == LANES - 1, beside, turned)
    beside = jnp.concatenate([turned[-1:], turned[:-1]], axis=0)
    return jnp.where(lane == 0, beside, turned)


def keep(value, x, row):
    if row >= 0 and row + value.shape[1] <= ROWS:
        return value
    at = lax.broadcasted_iota(jnp.int32, value.shape, 1) + (x * ROWS + row)
    return jnp.where((at >= 0) & (at < SPACES * ROWS), value, 0.0)


def potential(state, vort, slope, x, row, count=ROWS):
    rows = window(row, count)
    both = [state[layer, :, rows, :] for layer in range(2)]
    for layer in range(2):
        left, right = (shifted(state, layer, row, by, count) for by in (1, -1))
        above, below = (state[layer, :, window(row + by, count), :] for by in (-1, 1))
        value = (above + below) + (left + right) - (4.0 + COUPLE[layer]) * both[layer]
        value = value + COUPLE[layer] * both[1 - layer]
        vort[layer, :, rows, :] = keep(value, x, row)
        slope[layer, :, rows, :] = right - left


def first_sweep(state, vort, slope, target, half, force, pull, x, step_no, row):
    rows = window(row)
    for layer in range(2):
        here, q, ex_s = (ref[layer, :, rows, :] for ref in (state, vort, slope))
        ex_q = shifted(vort, layer, row, -1) - shifted(vort, layer, row, 1)
        ny_s, ny_q = (
            ref[layer, :, window(row + 1), :] - ref[layer, :, window(row - 1), :]
            for ref in (state, vort)
        )
        tendency = ny_s * ex_q - ex_s * (ny_q + 2.0 * BETA)
        change = (DT * 0.25) * tendency + force[step_no, layer, :, rows, :]
        if DRAG[layer]:
            change = change - (DT * DRAG[layer]) * q
        if layer == 0:
            change = change - pull[rows, :] * here
        target[layer, :, rows, :] = q + change
        value = here - change * (1.0 / (4.0 + COUPLE[layer]))
        half[layer, :, rows, :] = keep(value, x, row)


def second_sweep(half, target, x, row, put):
    rows = window(row)
    both = [half[layer, :, rows, :] for layer in range(2)]
    for layer in range(2):
        around = half[layer, :, window(row - 1), :] + half[layer, :, window(row + 1), :]
        around = around + shifted(half, layer, row, 1) + shifted(half, layer, row, -1)
        rest = around + COUPLE[layer] * both[1 - layer] - target[layer, :, rows, :]
        put(layer, keep(rest * (1.0 / (4.0 + COUPLE[layer])), x, row))


def kernel(
    offspring_in, new_owner_in, nudge_in, ensemble, perturb, observed, out,
    offspring, new_owner, nudge, noise, obs, tiles, picked, parent_row, parent_at,
    state, vort, slope, target, half, force, pull,
    local_sem, spread_send, spread_recv, deliver_send, deliver_recv,
    early_send, early_recv, row_send, row_recv, direct_send, direct_recv,
):
    me, x = lax.axis_index("dom"), lax.axis_index("space")
    plane, y, core = lax.div(me, 8), lax.rem(lax.div(me, 2), 4), lax.rem(me, 2)
    my_tile = lax.div(me, 2)
    places = [
        (lax.rem(y + dy, 4), lax.rem(core + dc, 2))
        for dy, dc in ((2, 1), (2, 0), (1, 1), (1, 0), (3, 1), (3, 0), (0, 1), (0, 0))
    ]

    def nth_plane(n):
        far = (n + 1) // 2
        return lax.rem(plane + jnp.where(n % 2 == 1, 4 - far, 4 + far), PLANES)

    def each_plane(act):
        def one_plane(n, carry):
            act(nth_plane(n), PER_PLANE)
            return carry

        lax.fori_loop(0, PLANES - 1, one_plane, 0)
        act(plane, PER_PLANE - 1)

    def each_partner(act):
        def in_plane(z, count):
            for at_y, at_core in places[:count]:
                act(z * PER_PLANE + at_y * 2 + at_core, z, at_y, at_core)

        each_plane(in_plane)

    loads = [
        pltpu.make_async_copy(new_owner_in, new_owner, local_sem.at[0]),
        pltpu.make_async_copy(offspring_in, offspring, local_sem.at[1]),
        pltpu.make_async_copy(nudge_in, nudge, local_sem.at[2]),
        pltpu.make_async_copy(perturb.at[0], noise, local_sem.at[3]),
        pltpu.make_async_copy(observed, obs, local_sem.at[4]),
    ]
    barrier = pltpu.get_barrier_semaphore()
    each_partner(lambda to, *_: pl.semaphore_signal(barrier, inc=1, device_id=(to, x)))

    has_prev, has_next = x > 0, x < SPACES - 1

    @pl.when(has_prev)
    def _():
        pl.semaphore_signal(barrier, inc=1, device_id=(me, x - 1))

    @pl.when(has_next)
    def _():
        pl.semaphore_signal(barrier, inc=1, device_id=(me, x + 1))

    for load in loads:
        load.start()
    beside = jnp.where(has_prev, 1, 0) + jnp.where(has_next, 1, 0)
    pl.semaphore_wait(barrier, MEMBERS - 1 + beside)

    own_tiles = []
    for part, (row, count) in enumerate(SPREAD):
        rows = pl.ds(row, count)

        def spread_to(to, z, at_y, at_core, part=part, rows=rows):
            start = pl.multiple_of((z * 4 + at_y) * LANES, LANES)
            pltpu.make_async_remote_copy(
                src_ref=ensemble.at[0, at_core, rows, pl.ds(start, LANES)],
                dst_ref=tiles[part].at[me, rows],
                send_sem=spread_send.at[part],
                recv_sem=spread_recv.at[part],
                device_id=(to, x),
            ).start()

        each_partner(spread_to)
        start = pl.multiple_of(my_tile * LANES, LANES)
        own = pltpu.make_async_copy(
            ensemble.at[0, core, rows, pl.ds(start, LANES)],
            tiles[part].at[me, rows],
            local_sem.at[5 + part],
        )
        own.start()
        own_tiles.append(own)

    for load in loads:
        load.wait()
    lane = lax.broadcasted_iota(jnp.int32, (8, LANES), 1)
    copy = jnp.zeros((8, LANES), jnp.int32)
    for j in range(MEMBERS):
        copy = jnp.where(lane == new_owner[j], j, copy)
    parent, total = jnp.zeros((8, LANES), jnp.int32), jnp.int32(0)
    for i in range(MEMBERS):
        total = total + offspring[i]
        parent = parent + (total <= copy).astype(jnp.int32)
    parent_row[...] = jnp.minimum(parent, MEMBERS - 1)
    to_scalars = pltpu.make_async_copy(parent_row, parent_at, local_sem.at[0])
    to_scalars.start()

    at = lax.broadcasted_iota(jnp.int32, (ROWS, LANES), 0)
    rate = jnp.zeros((ROWS, LANES), F32)
    for r in range(ROWS):
        rate = jnp.where(at == r, DT * nudge[r], rate)
    own_rows = window(0)
    pull[own_rows, :] = rate
    for tile in range(TILES):
        here = pl.ds(tile * LANES, LANES)
        drawn = rate * obs[:, here]
        for t in range(STEPS):
            for layer in range(2):
                value = NOISE * noise[t, layer, :, here].astype(F32)
                force[t, layer, tile, own_rows, :] = value + drawn if layer == 0 else value

    def row_copy(src, dst, send, recv, to_x):
        return pltpu.make_async_remote_copy(
            src_ref=src, dst_ref=dst, send_sem=send, recv_sem=recv, device_id=(me, to_x)
        )

    def early_copies(side):
        copies = []
        by, to_x = ((ROWS, x - 1), (-ROWS, x + 1))[side]
        for number, (row, count) in enumerate((((0, 4), (0, 1)), ((4, 4), (7, 1)))[side]):
            src, dst = window(row, count), window(row + by, count)
            copies.append((force.at[number, :, :, src, :], force.at[number, :, :, dst, :]))
            if number == 0:
                copies.append((pull.at[src, :], pull.at[dst, :]))
        return [
            row_copy(src, dst, early_send.at[side, n], early_recv.at[side, n], to_x)
            for n, (src, dst) in enumerate(copies)
        ]

    @pl.when(has_prev)
    def _():
        for one in early_copies(0):
            one.start()

    @pl.when(has_next)
    def _():
        for one in early_copies(1):
            one.start()

    to_scalars.wait()

    def tiles_of(row, count, number):
        some = tiles[0].at[pl.ds(0, number), pl.ds(row, count)]
        return lambda sem: pltpu.make_async_copy(some, some, sem).wait()

    def sides_of(row):
        sides = ((0, (ROWS, x - 1, has_prev)), (1, (-ROWS, x + 1, has_next)))
        return [sides[n] for n in (0, 1) if (row >= ROWS - HALO if n else row < HALO)]

    arrived = -1
    for part, (spread, row, count) in enumerate(PARTS):
        if spread > arrived:
            arrived = spread
            own_tiles[spread].wait()
            tiles_of(*SPREAD[spread], MEMBERS - 1)(spread_recv.at[spread])
        rows, lands = pl.ds(row, count), window(row, count)

        def deliver_in(
            z, count, part=part, spread=spread, row=row, size=count, rows=rows, lands=lands
        ):
            for place in range(PER_PLANE):
                m = z * PER_PLANE + place
                picked[part][m, rows] = tiles[spread][parent_at[0, m], rows]
            for at_y, at_core in places[:count]:
                to = z * PER_PLANE + at_y * 2 + at_core
                pltpu.make_async_remote_copy(
                    src_ref=picked[part].at[to, rows],
                    dst_ref=state.at[core, my_tile, lands, :],
                    send_sem=deliver_send.at[part],
                    recv_sem=deliver_recv.at[part, plane],
                    device_id=(to, x),
                ).start()
            if part in DIRECT:
                for side, (by, to_x, there) in sides_of(row):

                    @pl.when(there)
                    def _(side=side, by=by, to_x=to_x):
                        for at_y, at_core in places:
                            to = z * PER_PLANE + at_y * 2 + at_core
                            pltpu.make_async_remote_copy(
                                src_ref=picked[part].at[to, rows],
                                dst_ref=state.at[core, my_tile, window(row + by, size), :],
                                send_sem=direct_send.at[part],
                                recv_sem=direct_recv.at[part],
                                device_id=(to, to_x),
                            ).start()

        each_plane(deliver_in)
        state[core, my_tile, lands, :] = picked[part][me, rows]

    for part, (_, row, count) in enumerate(PARTS):

        def pass_on(z, number, part=part, row=row, count=count):
            tiles_of(row, count, number)(deliver_recv.at[part, z])
            band = pl.ds(z * BAND, BAND)
            for side, (by, to_x, there) in sides_of(row):
                if part not in DIRECT:

                    @pl.when(there)
                    def _(side=side, by=by, to_x=to_x):
                        row_copy(
                            state.at[:, band, window(row, count), :],
                            state.at[:, band, window(row + by, count), :],
                            row_send.at[side],
                            row_recv.at[side],
                            to_x,
                        ).start()

        each_plane(pass_on)

    passed = [
        sum(
            count
            for part, (_, row, count) in enumerate(PARTS)
            if part not in DIRECT and (row >= ROWS - HALO if side else row < HALO)
        )
        for side in (0, 1)
    ]

    def some_rows(side, sem):
        some = state.at[:, :, window(0, passed[side]), :]
        return pltpu.make_async_copy(some, some, sem.at[side])

    def direct_parts(side):
        return [p for p in DIRECT if side in [n for n, _ in sides_of(PARTS[p][1])]]

    def rows_from(side):
        for one in early_copies(side):
            one.wait_recv()
        some_rows(side, row_recv).wait()
        for part in direct_parts(side):
            tiles_of(*PARTS[part][1:], MEMBERS)(direct_recv.at[part])

    def no_rows(row):
        state[:, :, window(row, HALO), :] = jnp.zeros((2, TILES, HALO, LANES), F32)

    def one_side(q_row, s_row):
        potential(state, vort, slope, x, q_row)
        first_sweep(state, vort, slope, target, half, force, pull, x, 0, s_row)

    potential(state, vort, slope, x, 1, ROWS - 2)

    @pl.when(jnp.logical_not(has_prev))
    def _():
        no_rows(-HALO)
        one_side(-5, -4)

    @pl.when(has_next)
    def _():
        rows_from(0)

    @pl.when(jnp.logical_not(has_next))
    def _():
        no_rows(ROWS)

    one_side(5, 4)

    @pl.when(has_prev)
    def _():
        rows_from(1)
        one_side(-5, -4)

    for side, there in enumerate((has_prev, has_next)):

        @pl.when(there)
        def _(side=side):
            some_rows(side, row_send).wait()

    for row in (-3, 3):

        def put_state(layer, value, row=row):
            state[layer, :, window(row), :] = value

        second_sweep(half, target, x, row, put_state)

    for row in (-2, 2):
        potential(state, vort, slope, x, row)
    for row in (-1, 1):
        first_sweep(state, vort, slope, target, half, force, pull, x, 1, row)

    def put_out(layer, value):
        for tile in range(TILES):
            out[0, layer, :, pl.ds(tile * LANES, LANES)] = value[tile]

    second_sweep(half, target, x, 0, put_out)

    for part, rows in enumerate(SPREAD):
        tiles_of(*rows, MEMBERS - 1)(spread_send.at[part])
    for part, (_, *rows) in enumerate(PARTS):
        tiles_of(*rows, MEMBERS - 1)(deliver_send.at[part])
    for side, there in enumerate((has_prev, has_next)):

        @pl.when(there)
        def _(side=side):
            for one in early_copies(side):
                one.wait_send()
            for part in direct_parts(side):
                tiles_of(*PARTS[part][1:], MEMBERS)(direct_send.at[part])


def per_device(ensemble, offspring, new_owner, perturb, observed, nudge_rate):
    field = pltpu.VMEM((2, TILES, SPAN, LANES), F32)
    tiles = pltpu.VMEM((MEMBERS, 8, LANES), F32)
    dma = pltpu.SemaphoreType.DMA
    operands = [
        pltpu.with_memory_space_constraint(a, pltpu.HBM)
        for a in (offspring, new_owner, nudge_rate, ensemble, perturb, observed)
    ]
    return pl.pallas_call(
        kernel,
        out_shape=pltpu.VMEM(ensemble.shape, F32),
        in_specs=[pl.BlockSpec(memory_space=pltpu.HBM)] * 6,
        out_specs=pl.BlockSpec(memory_space=pltpu.VMEM),
        scratch_shapes=[
            pltpu.SMEM((MEMBERS,), jnp.int32),
            pltpu.SMEM((MEMBERS,), jnp.int32),
            pltpu.SMEM((ROWS,), F32),
            pltpu.VMEM((STEPS, 2, ROWS, COLS), jnp.bfloat16),
            pltpu.VMEM((ROWS, COLS), F32),
            [tiles] * len(SPREAD),
            [tiles] * len(PARTS),
            pltpu.VMEM((8, LANES), jnp.int32),
            pltpu.SMEM((8, LANES), jnp.int32),
            *[field] * 5,
            pltpu.VMEM((STEPS, 2, TILES, SPAN, LANES), F32),
            pltpu.VMEM((SPAN, LANES), F32),
            dma((5 + len(SPREAD),)),
            dma((len(SPREAD),)),
            dma((len(SPREAD),)),
            dma((len(PARTS),)),
            dma((len(PARTS), PLANES)),
            dma((2, 3)),
            dma((2, 3)),
            dma((2,)),
            dma((2,)),
            dma((len(PARTS),)),
            dma((len(PARTS),)),
        ],
        compiler_params=pltpu.CompilerParams(
            collective_id=0, has_side_effects=True, vmem_limit_bytes=48 * 1024 * 1024
        ),
        name="filter_step",
    )(*operands)


def solution(mesh):
    in_specs = (
        P("dom", None, "space", None),
        P(),
        P(),
        P("dom", None, None, "space", None),
        P("space", None),
        P("space"),
    )
    out_specs = P("dom", None, "space", None)
    return jax.shard_map(
        per_device, mesh=mesh, in_specs=in_specs, out_specs=out_specs, check_vma=False
    )
```

```python
import jax
import jax.numpy as jnp
from jax import lax
from jax.experimental import pallas as pl
from jax.experimental.pallas import tpu as pltpu
from jax.sharding import PartitionSpec as P

STEPS = 2
COLS = 4096
ROWS = 8
SPACES = 4
MEMBERS = 64
LANES = 128
TILES = COLS // LANES
PLANES = 8
PER_PLANE = 8
BAND = TILES // PLANES
SPAN = 3 * ROWS
HALO = 6
SPREAD = ((2, 2), (4, 2), (0, 2), (6, 2))
DELIVER = (((2, 2),), ((4, 2),), ((0, 2),), ((6, 2),))
PARTS = [(spread, *rows) for spread, parts in enumerate(DELIVER) for rows in parts]
DIRECT = (2, 3)
COUPLE = (0.4, 0.6)
DRAG = (0.0, 0.2)
DT = 0.05
BETA = 1.0
NOISE = 0.5
F32 = jnp.float32


def window(row, count=ROWS):
    return pl.ds(ROWS + row, count)


def shifted(ref, layer, row, by, count=ROWS):
    turned = pltpu.roll(ref[layer, :, window(row, count), :], by % LANES, 2)
    lane = lax.broadcasted_iota(jnp.int32, turned.shape, 2)
    if by < 0:
        beside = jnp.concatenate([turned[1:], turned[:1]], axis=0)
        return jnp.where(lane == LANES - 1, beside, turned)
    beside = jnp.concatenate([turned[-1:], turned[:-1]], axis=0)
    return jnp.where(lane == 0, beside, turned)


def keep(value, x, row):
    if row >= 0 and row + value.shape[1] <= ROWS:
        return value
    at = lax.broadcasted_iota(jnp.int32, value.shape, 1) + (x * ROWS + row)
    return jnp.where((at >= 0) & (at < SPACES * ROWS), value, 0.0)


def potential(state, vort, slope, x, row, count=ROWS):
    rows = window(row, count)
    both = [state[layer, :, rows, :] for layer in range(2)]
    for layer in range(2):
        left, right = (shifted(state, layer, row, by, count) for by in (1, -1))
        above, below = (state[layer, :, window(row + by, count), :] for by in (-1, 1))
        value = (above + below) + (left + right) - (4.0 + COUPLE[layer]) * both[layer]
        value = value + COUPLE[layer] * both[1 - layer]
        vort[layer, :, rows, :] = keep(value, x, row)
        slope[layer, :, rows, :] = right - left


def first_sweep(state, vort, slope, target, half, force, pull, x, step_no, row):
    rows = window(row)
    for layer in range(2):
        here, q, ex_s = (ref[layer, :, rows, :] for ref in (state, vort, slope))
        ex_q = shifted(vort, layer, row, -1) - shifted(vort, layer, row, 1)
        ny_s, ny_q = (
            ref[layer, :, window(row + 1), :] - ref[layer, :, window(row - 1), :]
            for ref in (state, vort)
        )
        tendency = ny_s * ex_q - ex_s * (ny_q + 2.0 * BETA)
        change = (DT * 0.25) * tendency + force[step_no, layer, :, rows, :]
        if DRAG[layer]:
            change = change - (DT * DRAG[layer]) * q
        if layer == 0:
            change = change - pull[rows, :] * here
        target[layer, :, rows, :] = q + change
        value = here - change * (1.0 / (4.0 + COUPLE[layer]))
        half[layer, :, rows, :] = keep(value, x, row)


def second_sweep(half, target, x, row, put):
    rows = window(row)
    both = [half[layer, :, rows, :] for layer in range(2)]
    for layer in range(2):
        around = half[layer, :, window(row - 1), :] + half[layer, :, window(row + 1), :]
        around = around + shifted(half, layer, row, 1) + shifted(half, layer, row, -1)
        rest = around + COUPLE[layer] * both[1 - layer] - target[layer, :, rows, :]
        put(layer, keep(rest * (1.0 / (4.0 + COUPLE[layer])), x, row))


def kernel(
    offspring_in, new_owner_in, nudge_in, ensemble, perturb, observed, out,
    offspring, new_owner, nudge, noise, obs, tiles, picked, parent_row, parent_at,
    state, vort, slope, target, half, force, pull,
    local_sem, spread_send, spread_recv, deliver_send, deliver_recv,
    early_send, early_recv, row_send, row_recv, direct_send, direct_recv,
):
    me, x = lax.axis_index("dom"), lax.axis_index("space")
    plane, y, core = lax.div(me, 8), lax.rem(lax.div(me, 2), 4), lax.rem(me, 2)
    my_tile = lax.div(me, 2)
    places = [
        (lax.rem(y + dy, 4), lax.rem(core + dc, 2))
        for dy, dc in ((2, 1), (2, 0), (1, 1), (1, 0), (3, 1), (3, 0), (0, 1), (0, 0))
    ]

    def nth_plane(n):
        far = (n + 1) // 2
        return lax.rem(plane + jnp.where(n % 2 == 1, 4 - far, 4 + far), PLANES)

    def each_plane(act):
        def one_plane(n, carry):
            act(nth_plane(n), PER_PLANE)
            return carry

        lax.fori_loop(0, PLANES - 1, one_plane, 0)
        act(plane, PER_PLANE - 1)

    def each_partner(act):
        def in_plane(z, count):
            for at_y, at_core in places[:count]:
                act(z * PER_PLANE + at_y * 2 + at_core, z, at_y, at_core)

        each_plane(in_plane)

    loads = [
        pltpu.make_async_copy(new_owner_in, new_owner, local_sem.at[0]),
        pltpu.make_async_copy(offspring_in, offspring, local_sem.at[1]),
        pltpu.make_async_copy(nudge_in, nudge, local_sem.at[2]),
        pltpu.make_async_copy(perturb.at[0], noise, local_sem.at[3]),
        pltpu.make_async_copy(observed, obs, local_sem.at[4]),
    ]
    barrier = pltpu.get_barrier_semaphore()
    each_partner(lambda to, *_: pl.semaphore_signal(barrier, inc=1, device_id=(to, x)))

    has_prev, has_next = x > 0, x < SPACES - 1
    prev_x, next_x = jnp.maximum(x - 1, 0), jnp.minimum(x + 1, SPACES - 1)

    @pl.when(has_prev)
    def _():
        pl.semaphore_signal(barrier, inc=1, device_id=(me, prev_x))

    @pl.when(has_next)
    def _():
        pl.semaphore_signal(barrier, inc=1, device_id=(me, next_x))

    for load in loads:
        load.start()
    beside = jnp.where(has_prev, 1, 0) + jnp.where(has_next, 1, 0)
    pl.semaphore_wait(barrier, MEMBERS - 1 + beside)

    own_tiles = []
    for part, (row, count) in enumerate(SPREAD):
        rows = pl.ds(row, count)

        def spread_to(to, z, at_y, at_core, part=part, rows=rows):
            start = pl.multiple_of((z * 4 + at_y) * LANES, LANES)
            pltpu.make_async_remote_copy(
                src_ref=ensemble.at[0, at_core, rows, pl.ds(start, LANES)],
                dst_ref=tiles[part].at[me, rows],
                send_sem=spread_send.at[part],
                recv_sem=spread_recv.at[part],
                device_id=(to, x),
            ).start()

        each_partner(spread_to)
        start = pl.multiple_of(my_tile * LANES, LANES)
        own = pltpu.make_async_copy(
            ensemble.at[0, core, rows, pl.ds(start, LANES)],
            tiles[part].at[me, rows],
            local_sem.at[5 + part],
        )
        own.start()
        own_tiles.append(own)

    for load in loads:
        load.wait()
    lane = lax.broadcasted_iota(jnp.int32, (8, LANES), 1)
    copy = jnp.zeros((8, LANES), jnp.int32)
    for j in range(MEMBERS):
        copy = jnp.where(lane == new_owner[j], j, copy)
    parent, total = jnp.zeros((8, LANES), jnp.int32), jnp.int32(0)
    for i in range(MEMBERS):
        total = total + offspring[i]
        parent = parent + (total <= copy).astype(jnp.int32)
    parent_row[...] = jnp.minimum(parent, MEMBERS - 1)
    to_scalars = pltpu.make_async_copy(parent_row, parent_at, local_sem.at[0])
    to_scalars.start()

    at = lax.broadcasted_iota(jnp.int32, (ROWS, LANES), 0)
    rate = jnp.zeros((ROWS, LANES), F32)
    for r in range(ROWS):
        rate = jnp.where(at == r, DT * nudge[r], rate)
    own_rows = window(0)
    pull[own_rows, :] = rate
    for tile in range(TILES):
        here = pl.ds(tile * LANES, LANES)
        drawn = rate * obs[:, here]
        for t in range(STEPS):
            for layer in range(2):
                value = NOISE * noise[t, layer, :, here].astype(F32)
                force[t, layer, tile, own_rows, :] = value + drawn if layer == 0 else value

    def row_copy(src, dst, send, recv, to_x):
        return pltpu.make_async_remote_copy(
            src_ref=src, dst_ref=dst, send_sem=send, recv_sem=recv, device_id=(me, to_x)
        )

    def early_copies(side):
        copies = []
        by, to_x = ((ROWS, prev_x), (-ROWS, next_x))[side]
        for number, (row, count) in enumerate((((0, 4), (0, 1)), ((4, 4), (7, 1)))[side]):
            src, dst = window(row, count), window(row + by, count)
            copies.append((force.at[number, :, :, src, :], force.at[number, :, :, dst, :]))
            if number == 0:
                copies.append((pull.at[src, :], pull.at[dst, :]))
        return [
            row_copy(src, dst, early_send.at[side, n], early_recv.at[side, n], to_x)
            for n, (src, dst) in enumerate(copies)
        ]

    @pl.when(has_prev)
    def _():
        for one in early_copies(0):
            one.start()

    @pl.when(has_next)
    def _():
        for one in early_copies(1):
            one.start()

    to_scalars.wait()

    def tiles_of(row, count, number):
        some = tiles[0].at[pl.ds(0, number), pl.ds(row, count)]
        return lambda sem: pltpu.make_async_copy(some, some, sem).wait()

    def sides_of(row):
        sides = ((0, (ROWS, prev_x, has_prev)), (1, (-ROWS, next_x, has_next)))
        return [sides[n] for n in (0, 1) if (row >= ROWS - HALO if n else row < HALO)]

    arrived = -1
    for part, (spread, row, count) in enumerate(PARTS):
        if spread > arrived:
            arrived = spread
            own_tiles[spread].wait()
            tiles_of(*SPREAD[spread], MEMBERS - 1)(spread_recv.at[spread])
        rows, lands = pl.ds(row, count), window(row, count)

        def deliver_in(
            z, count, part=part, spread=spread, row=row, size=count, rows=rows, lands=lands
        ):
            for place in range(PER_PLANE):
                m = z * PER_PLANE + place
                picked[part][m, rows] = tiles[spread][parent_at[0, m], rows]
            for at_y, at_core in places[:count]:
                to = z * PER_PLANE + at_y * 2 + at_core
                pltpu.make_async_remote_copy(
                    src_ref=picked[part].at[to, rows],
                    dst_ref=state.at[core, my_tile, lands, :],
                    send_sem=deliver_send.at[part],
                    recv_sem=deliver_recv.at[part, 0 if part in DIRECT else plane],
                    device_id=(to, x),
                ).start()
            if part in DIRECT:
                for side, (by, to_x, there) in sides_of(row):

                    @pl.when(there)
                    def _(side=side, by=by, to_x=to_x):
                        for at_y, at_core in places:
                            to = z * PER_PLANE + at_y * 2 + at_core
                            pltpu.make_async_remote_copy(
                                src_ref=picked[part].at[to, rows],
                                dst_ref=state.at[core, my_tile, window(row + by, size), :],
                                send_sem=direct_send.at[part],
                                recv_sem=direct_recv.at[part],
                                device_id=(to, to_x),
                            ).start()

        each_plane(deliver_in)
        state[core, my_tile, lands, :] = picked[part][me, rows]

    for part, (_, row, count) in enumerate(PARTS):

        def pass_on(z, number, part=part, row=row, count=count):
            tiles_of(row, count, number)(deliver_recv.at[part, z])
            band = pl.ds(z * BAND, BAND)
            for side, (by, to_x, there) in sides_of(row):

                @pl.when(there)
                def _(side=side, by=by, to_x=to_x):
                    row_copy(
                        state.at[:, band, window(row, count), :],
                        state.at[:, band, window(row + by, count), :],
                        row_send.at[side],
                        row_recv.at[side],
                        to_x,
                    ).start()

        if part in DIRECT:
            tiles_of(row, count, MEMBERS - 1)(deliver_recv.at[part, 0])
        else:
            each_plane(pass_on)

    passed = [
        sum(
            count
            for part, (_, row, count) in enumerate(PARTS)
            if part not in DIRECT and (row >= ROWS - HALO if side else row < HALO)
        )
        for side in (0, 1)
    ]

    def some_rows(side, sem):
        some = state.at[:, :, window(0, passed[side]), :]
        return pltpu.make_async_copy(some, some, sem.at[side])

    def direct_parts(side):
        return [p for p in DIRECT if side in [n for n, _ in sides_of(PARTS[p][1])]]

    def rows_from(side):
        for one in early_copies(side):
            one.wait_recv()
        some_rows(side, row_recv).wait()
        for part in direct_parts(side):
            tiles_of(*PARTS[part][1:], MEMBERS)(direct_recv.at[part])

    def no_rows(row):
        state[:, :, window(row, HALO), :] = jnp.zeros((2, TILES, HALO, LANES), F32)

    def one_side(q_row, s_row):
        potential(state, vort, slope, x, q_row)
        first_sweep(state, vort, slope, target, half, force, pull, x, 0, s_row)

    potential(state, vort, slope, x, 1, ROWS - 2)

    @pl.when(jnp.logical_not(has_prev))
    def _():
        no_rows(-HALO)
        one_side(-5, -4)

    @pl.when(has_next)
    def _():
        rows_from(0)

    @pl.when(jnp.logical_not(has_next))
    def _():
        no_rows(ROWS)

    one_side(5, 4)

    @pl.when(has_prev)
    def _():
        rows_from(1)
        one_side(-5, -4)

    for side, there in enumerate((has_prev, has_next)):

        @pl.when(there)
        def _(side=side):
            some_rows(side, row_send).wait()

    for row in (-3, 3):

        def put_state(layer, value, row=row):
            state[layer, :, window(row), :] = value

        second_sweep(half, target, x, row, put_state)

    for row in (-2, 2):
        potential(state, vort, slope, x, row)
    for row in (-1, 1):
        first_sweep(state, vort, slope, target, half, force, pull, x, 1, row)

    def put_out(layer, value):
        for tile in range(TILES):
            out[0, layer, :, pl.ds(tile * LANES, LANES)] = value[tile]

    second_sweep(half, target, x, 0, put_out)

    for part, rows in enumerate(SPREAD):
        tiles_of(*rows, MEMBERS - 1)(spread_send.at[part])
    for part, (_, *rows) in enumerate(PARTS):
        tiles_of(*rows, MEMBERS - 1)(deliver_send.at[part])
    for side, there in enumerate((has_prev, has_next)):

        @pl.when(there)
        def _(side=side):
            for one in early_copies(side):
                one.wait_send()
            for part in direct_parts(side):
                tiles_of(*PARTS[part][1:], MEMBERS)(direct_send.at[part])


def per_device(ensemble, offspring, new_owner, perturb, observed, nudge_rate):
    field = pltpu.VMEM((2, TILES, SPAN, LANES), F32)
    tiles = pltpu.VMEM((MEMBERS, 8, LANES), F32)
    dma = pltpu.SemaphoreType.DMA
    operands = [
        pltpu.with_memory_space_constraint(a, pltpu.HBM)
        for a in (offspring, new_owner, nudge_rate, ensemble, perturb, observed)
    ]
    return pl.pallas_call(
        kernel,
        out_shape=pltpu.VMEM(ensemble.shape, F32),
        in_specs=[pl.BlockSpec(memory_space=pltpu.HBM)] * 6,
        out_specs=pl.BlockSpec(memory_space=pltpu.VMEM),
        scratch_shapes=[
            pltpu.SMEM((MEMBERS,), jnp.int32),
            pltpu.SMEM((MEMBERS,), jnp.int32),
            pltpu.SMEM((ROWS,), F32),
            pltpu.VMEM((STEPS, 2, ROWS, COLS), jnp.bfloat16),
            pltpu.VMEM((ROWS, COLS), F32),
            [tiles] * len(SPREAD),
            [tiles] * len(PARTS),
            pltpu.VMEM((8, LANES), jnp.int32),
            pltpu.SMEM((8, LANES), jnp.int32),
            *[field] * 5,
            pltpu.VMEM((STEPS, 2, TILES, SPAN, LANES), F32),
            pltpu.VMEM((SPAN, LANES), F32),
            dma((5 + len(SPREAD),)),
            dma((len(SPREAD),)),
            dma((len(SPREAD),)),
            dma((len(PARTS),)),
            dma((len(PARTS), PLANES)),
            dma((2, 3)),
            dma((2, 3)),
            dma((2,)),
            dma((2,)),
            dma((len(PARTS),)),
            dma((len(PARTS),)),
        ],
        compiler_params=pltpu.CompilerParams(
            collective_id=0, has_side_effects=True, vmem_limit_bytes=48 * 1024 * 1024
        ),
        name="filter_step",
    )(*operands)


def solution(mesh):
    in_specs = (
        P("dom", None, "space", None),
        P(),
        P(),
        P("dom", None, None, "space", None),
        P("space", None),
        P("space"),
    )
    out_specs = P("dom", None, "space", None)
    return jax.shard_map(
        per_device, mesh=mesh, in_specs=in_specs, out_specs=out_specs, check_vma=False
    )
```

```python
import jax
import jax.numpy as jnp
from jax import lax
from jax.experimental import pallas as pl
from jax.experimental.pallas import tpu as pltpu
from jax.sharding import PartitionSpec as P

STEPS = 2
COLS = 4096
ROWS = 8
SPACES = 4
MEMBERS = 64
LANES = 128
TILES = COLS // LANES
PLANES = 8
PER_PLANE = 8
BAND = TILES // PLANES
SPAN = 3 * ROWS
HALO = 6
SPREAD = ((2, 2), (4, 2), (1, 1), (6, 1), (0, 1), (7, 1))
DELIVER = tuple((p,) for p in SPREAD)
PARTS = [(spread, *rows) for spread, parts in enumerate(DELIVER) for rows in parts]
DIRECT = (4, 5)
COUPLE = (0.4, 0.6)
DRAG = (0.0, 0.2)
DT = 0.05
BETA = 1.0
NOISE = 0.5
F32 = jnp.float32


def window(row, count=ROWS):
    return pl.ds(ROWS + row, count)


def shifted(ref, layer, row, by, count=ROWS):
    turned = pltpu.roll(ref[layer, :, window(row, count), :], by % LANES, 2)
    lane = lax.broadcasted_iota(jnp.int32, turned.shape, 2)
    if by < 0:
        beside = jnp.concatenate([turned[1:], turned[:1]], axis=0)
        return jnp.where(lane == LANES - 1, beside, turned)
    beside = jnp.concatenate([turned[-1:], turned[:-1]], axis=0)
    return jnp.where(lane == 0, beside, turned)


def keep(value, x, row):
    if row >= 0 and row + value.shape[1] <= ROWS:
        return value
    at = lax.broadcasted_iota(jnp.int32, value.shape, 1) + (x * ROWS + row)
    return jnp.where((at >= 0) & (at < SPACES * ROWS), value, 0.0)


def potential(state, vort, slope, x, row, count=ROWS):
    rows = window(row, count)
    both = [state[layer, :, rows, :] for layer in range(2)]
    for layer in range(2):
        left, right = (shifted(state, layer, row, by, count) for by in (1, -1))
        above, below = (state[layer, :, window(row + by, count), :] for by in (-1, 1))
        value = (above + below) + (left + right) - (4.0 + COUPLE[layer]) * both[layer]
        value = value + COUPLE[layer] * both[1 - layer]
        vort[layer, :, rows, :] = keep(value, x, row)
        slope[layer, :, rows, :] = right - left


def first_sweep(state, vort, slope, target, half, force, pull, x, step_no, row):
    rows = window(row)
    for layer in range(2):
        here, q, ex_s = (ref[layer, :, rows, :] for ref in (state, vort, slope))
        ex_q = shifted(vort, layer, row, -1) - shifted(vort, layer, row, 1)
        ny_s, ny_q = (
            ref[layer, :, window(row + 1), :] - ref[layer, :, window(row - 1), :]
            for ref in (state, vort)
        )
        tendency = ny_s * ex_q - ex_s * (ny_q + 2.0 * BETA)
        change = (DT * 0.25) * tendency + force[step_no, layer, :, rows, :]
        if DRAG[layer]:
            change = change - (DT * DRAG[layer]) * q
        if layer == 0:
            change = change - pull[rows, :] * here
        target[layer, :, rows, :] = q + change
        value = here - change * (1.0 / (4.0 + COUPLE[layer]))
        half[layer, :, rows, :] = keep(value, x, row)


def second_sweep(half, target, x, row, put):
    rows = window(row)
    both = [half[layer, :, rows, :] for layer in range(2)]
    for layer in range(2):
        around = half[layer, :, window(row - 1), :] + half[layer, :, window(row + 1), :]
        around = around + shifted(half, layer, row, 1) + shifted(half, layer, row, -1)
        rest = around + COUPLE[layer] * both[1 - layer] - target[layer, :, rows, :]
        put(layer, keep(rest * (1.0 / (4.0 + COUPLE[layer])), x, row))


def kernel(
    offspring_in, new_owner_in, nudge_in, ensemble, perturb, observed, out,
    offspring, new_owner, nudge, noise, obs, tiles, picked, parent_row, parent_at,
    state, vort, slope, target, half, force, pull,
    local_sem, spread_send, spread_recv, deliver_send, deliver_recv,
    early_send, early_recv, row_send, row_recv, direct_send, direct_recv,
):
    me, x = lax.axis_index("dom"), lax.axis_index("space")
    plane, y, core = lax.div(me, 8), lax.rem(lax.div(me, 2), 4), lax.rem(me, 2)
    my_tile = lax.div(me, 2)
    places = [
        (lax.rem(y + dy, 4), lax.rem(core + dc, 2))
        for dy, dc in ((2, 1), (2, 0), (1, 1), (1, 0), (3, 1), (3, 0), (0, 1), (0, 0))
    ]

    def nth_plane(n):
        far = (n + 1) // 2
        return lax.rem(plane + jnp.where(n % 2 == 1, 4 - far, 4 + far), PLANES)

    def each_plane(act):
        def one_plane(n, carry):
            act(nth_plane(n), PER_PLANE)
            return carry

        lax.fori_loop(0, PLANES - 1, one_plane, 0)
        act(plane, PER_PLANE - 1)

    def each_partner(act):
        def in_plane(z, count):
            for at_y, at_core in places[:count]:
                act(z * PER_PLANE + at_y * 2 + at_core, z, at_y, at_core)

        each_plane(in_plane)

    loads = [
        pltpu.make_async_copy(new_owner_in, new_owner, local_sem.at[0]),
        pltpu.make_async_copy(offspring_in, offspring, local_sem.at[1]),
        pltpu.make_async_copy(nudge_in, nudge, local_sem.at[2]),
        pltpu.make_async_copy(perturb.at[0], noise, local_sem.at[3]),
        pltpu.make_async_copy(observed, obs, local_sem.at[4]),
    ]
    barrier = pltpu.get_barrier_semaphore()
    each_partner(lambda to, *_: pl.semaphore_signal(barrier, inc=1, device_id=(to, x)))

    has_prev, has_next = x > 0, x < SPACES - 1
    prev_x, next_x = jnp.maximum(x - 1, 0), jnp.minimum(x + 1, SPACES - 1)

    @pl.when(has_prev)
    def _():
        pl.semaphore_signal(barrier, inc=1, device_id=(me, prev_x))

    @pl.when(has_next)
    def _():
        pl.semaphore_signal(barrier, inc=1, device_id=(me, next_x))

    for load in loads:
        load.start()
    beside = jnp.where(has_prev, 1, 0) + jnp.where(has_next, 1, 0)
    pl.semaphore_wait(barrier, MEMBERS - 1 + beside)

    own_tiles = []
    for part, (row, count) in enumerate(SPREAD):
        rows = pl.ds(row, count)

        def spread_to(to, z, at_y, at_core, part=part, rows=rows):
            start = pl.multiple_of((z * 4 + at_y) * LANES, LANES)
            pltpu.make_async_remote_copy(
                src_ref=ensemble.at[0, at_core, rows, pl.ds(start, LANES)],
                dst_ref=tiles[part].at[me, rows],
                send_sem=spread_send.at[part],
                recv_sem=spread_recv.at[part],
                device_id=(to, x),
            ).start()

        each_partner(spread_to)
        start = pl.multiple_of(my_tile * LANES, LANES)
        own = pltpu.make_async_copy(
            ensemble.at[0, core, rows, pl.ds(start, LANES)],
            tiles[part].at[me, rows],
            local_sem.at[5 + part],
        )
        own.start()
        own_tiles.append(own)

    for load in loads:
        load.wait()
    lane = lax.broadcasted_iota(jnp.int32, (8, LANES), 1)
    copy = jnp.zeros((8, LANES), jnp.int32)
    for j in range(MEMBERS):
        copy = jnp.where(lane == new_owner[j], j, copy)
    parent, total = jnp.zeros((8, LANES), jnp.int32), jnp.int32(0)
    for i in range(MEMBERS):
        total = total + offspring[i]
        parent = parent + (total <= copy).astype(jnp.int32)
    parent_row[...] = jnp.minimum(parent, MEMBERS - 1)
    to_scalars = pltpu.make_async_copy(parent_row, parent_at, local_sem.at[0])
    to_scalars.start()

    at = lax.broadcasted_iota(jnp.int32, (ROWS, LANES), 0)
    rate = jnp.zeros((ROWS, LANES), F32)
    for r in range(ROWS):
        rate = jnp.where(at == r, DT * nudge[r], rate)
    own_rows = window(0)
    pull[own_rows, :] = rate
    for tile in range(TILES):
        here = pl.ds(tile * LANES, LANES)
        drawn = rate * obs[:, here]
        for t in range(STEPS):
            for layer in range(2):
                value = NOISE * noise[t, layer, :, here].astype(F32)
                force[t, layer, tile, own_rows, :] = value + drawn if layer == 0 else value

    def row_copy(src, dst, send, recv, to_x):
        return pltpu.make_async_remote_copy(
            src_ref=src, dst_ref=dst, send_sem=send, recv_sem=recv, device_id=(me, to_x)
        )

    def early_copies(side):
        copies = []
        by, to_x = ((ROWS, prev_x), (-ROWS, next_x))[side]
        for number, (row, count) in enumerate((((0, 4), (0, 1)), ((4, 4), (7, 1)))[side]):
            src, dst = window(row, count), window(row + by, count)
            copies.append((force.at[number, :, :, src, :], force.at[number, :, :, dst, :]))
            if number == 0:
                copies.append((pull.at[src, :], pull.at[dst, :]))
        return [
            row_copy(src, dst, early_send.at[side, n], early_recv.at[side, n], to_x)
            for n, (src, dst) in enumerate(copies)
        ]

    @pl.when(has_prev)
    def _():
        for one in early_copies(0):
            one.start()

    @pl.when(has_next)
    def _():
        for one in early_copies(1):
            one.start()

    to_scalars.wait()

    def tiles_of(row, count, number):
        some = tiles[0].at[pl.ds(0, number), pl.ds(row, count)]
        return lambda sem: pltpu.make_async_copy(some, some, sem).wait()

    def sides_of(row):
        sides = ((0, (ROWS, prev_x, has_prev)), (1, (-ROWS, next_x, has_next)))
        return [sides[n] for n in (0, 1) if (row >= ROWS - HALO if n else row < HALO)]

    arrived = -1
    for part, (spread, row, count) in enumerate(PARTS):
        if spread > arrived:
            arrived = spread
            own_tiles[spread].wait()
            tiles_of(*SPREAD[spread], MEMBERS - 1)(spread_recv.at[spread])
        rows, lands = pl.ds(row, count), window(row, count)

        def deliver_in(
            z, count, part=part, spread=spread, row=row, size=count, rows=rows, lands=lands
        ):
            for place in range(PER_PLANE):
                m = z * PER_PLANE + place
                picked[part][m, rows] = tiles[spread][parent_at[0, m], rows]
            if part in DIRECT:
                for side, (by, to_x, there) in sides_of(row):

                    @pl.when(there)
                    def _(side=side, by=by, to_x=to_x):
                        for at_y, at_core in places:
                            to = z * PER_PLANE + at_y * 2 + at_core
                            pltpu.make_async_remote_copy(
                                src_ref=picked[part].at[to, rows],
                                dst_ref=state.at[core, my_tile, window(row + by, size), :],
                                send_sem=direct_send.at[part],
                                recv_sem=direct_recv.at[part],
                                device_id=(to, to_x),
                            ).start()
            for at_y, at_core in places[:count]:
                to = z * PER_PLANE + at_y * 2 + at_core
                pltpu.make_async_remote_copy(
                    src_ref=picked[part].at[to, rows],
                    dst_ref=state.at[core, my_tile, lands, :],
                    send_sem=deliver_send.at[part],
                    recv_sem=deliver_recv.at[part, 0 if part in DIRECT else plane],
                    device_id=(to, x),
                ).start()

        each_plane(deliver_in)
        state[core, my_tile, lands, :] = picked[part][me, rows]

    for part, (_, row, count) in enumerate(PARTS):

        def pass_on(z, number, part=part, row=row, count=count):
            tiles_of(row, count, number)(deliver_recv.at[part, z])
            band = pl.ds(z * BAND, BAND)
            for side, (by, to_x, there) in sides_of(row):

                @pl.when(there)
                def _(side=side, by=by, to_x=to_x):
                    row_copy(
                        state.at[:, band, window(row, count), :],
                        state.at[:, band, window(row + by, count), :],
                        row_send.at[side],
                        row_recv.at[side],
                        to_x,
                    ).start()

        if part in DIRECT:
            tiles_of(row, count, MEMBERS - 1)(deliver_recv.at[part, 0])
        else:
            each_plane(pass_on)

    passed = [
        sum(
            count
            for part, (_, row, count) in enumerate(PARTS)
            if part not in DIRECT and (row >= ROWS - HALO if side else row < HALO)
        )
        for side in (0, 1)
    ]

    def some_rows(side, sem):
        some = state.at[:, :, window(0, passed[side]), :]
        return pltpu.make_async_copy(some, some, sem.at[side])

    def direct_parts(side):
        return [p for p in DIRECT if side in [n for n, _ in sides_of(PARTS[p][1])]]

    def rows_from(side):
        for one in early_copies(side):
            one.wait_recv()
        some_rows(side, row_recv).wait()
        for part in direct_parts(side):
            tiles_of(*PARTS[part][1:], MEMBERS)(direct_recv.at[part])

    def no_rows(row):
        state[:, :, window(row, HALO), :] = jnp.zeros((2, TILES, HALO, LANES), F32)

    def one_side(q_row, s_row):
        potential(state, vort, slope, x, q_row)
        first_sweep(state, vort, slope, target, half, force, pull, x, 0, s_row)

    potential(state, vort, slope, x, 1, ROWS - 2)

    @pl.when(jnp.logical_not(has_prev))
    def _():
        no_rows(-HALO)
        one_side(-5, -4)

    @pl.when(has_next)
    def _():
        rows_from(0)

    @pl.when(jnp.logical_not(has_next))
    def _():
        no_rows(ROWS)

    one_side(5, 4)

    @pl.when(has_prev)
    def _():
        rows_from(1)
        one_side(-5, -4)

    for side, there in enumerate((has_prev, has_next)):

        @pl.when(there)
        def _(side=side):
            some_rows(side, row_send).wait()

    for row in (-3, 3):

        def put_state(layer, value, row=row):
            state[layer, :, window(row), :] = value

        second_sweep(half, target, x, row, put_state)

    for row in (-2, 2):
        potential(state, vort, slope, x, row)
    for row in (-1, 1):
        first_sweep(state, vort, slope, target, half, force, pull, x, 1, row)

    def put_out(layer, value):
        for tile in range(TILES):
            out[0, layer, :, pl.ds(tile * LANES, LANES)] = value[tile]

    second_sweep(half, target, x, 0, put_out)

    for part, rows in enumerate(SPREAD):
        tiles_of(*rows, MEMBERS - 1)(spread_send.at[part])
    for part, (_, *rows) in enumerate(PARTS):
        tiles_of(*rows, MEMBERS - 1)(deliver_send.at[part])
    for side, there in enumerate((has_prev, has_next)):

        @pl.when(there)
        def _(side=side):
            for one in early_copies(side):
                one.wait_send()
            for part in direct_parts(side):
                tiles_of(*PARTS[part][1:], MEMBERS)(direct_send.at[part])


def per_device(ensemble, offspring, new_owner, perturb, observed, nudge_rate):
    field = pltpu.VMEM((2, TILES, SPAN, LANES), F32)
    tiles = pltpu.VMEM((MEMBERS, 8, LANES), F32)
    dma = pltpu.SemaphoreType.DMA
    operands = [
        pltpu.with_memory_space_constraint(a, pltpu.HBM)
        for a in (offspring, new_owner, nudge_rate, ensemble, perturb, observed)
    ]
    return pl.pallas_call(
        kernel,
        out_shape=pltpu.VMEM(ensemble.shape, F32),
        in_specs=[pl.BlockSpec(memory_space=pltpu.HBM)] * 6,
        out_specs=pl.BlockSpec(memory_space=pltpu.VMEM),
        scratch_shapes=[
            pltpu.SMEM((MEMBERS,), jnp.int32),
            pltpu.SMEM((MEMBERS,), jnp.int32),
            pltpu.SMEM((ROWS,), F32),
            pltpu.VMEM((STEPS, 2, ROWS, COLS), jnp.bfloat16),
            pltpu.VMEM((ROWS, COLS), F32),
            [tiles] * len(SPREAD),
            [tiles] * len(PARTS),
            pltpu.VMEM((8, LANES), jnp.int32),
            pltpu.SMEM((8, LANES), jnp.int32),
            *[field] * 5,
            pltpu.VMEM((STEPS, 2, TILES, SPAN, LANES), F32),
            pltpu.VMEM((SPAN, LANES), F32),
            dma((5 + len(SPREAD),)),
            dma((len(SPREAD),)),
            dma((len(SPREAD),)),
            dma((len(PARTS),)),
            dma((len(PARTS), PLANES)),
            dma((2, 3)),
            dma((2, 3)),
            dma((2,)),
            dma((2,)),
            dma((len(PARTS),)),
            dma((len(PARTS),)),
        ],
        compiler_params=pltpu.CompilerParams(
            collective_id=0, has_side_effects=True, vmem_limit_bytes=48 * 1024 * 1024
        ),
        name="filter_step",
    )(*operands)


def solution(mesh):
    in_specs = (
        P("dom", None, "space", None),
        P(),
        P(),
        P("dom", None, None, "space", None),
        P("space", None),
        P("space"),
    )
    out_specs = P("dom", None, "space", None)
    return jax.shard_map(
        per_device, mesh=mesh, in_specs=in_specs, out_specs=out_specs, check_vma=False
    )
```
